32 devices in a mesh: energy: 16 (over z, y, core), space: 2 (over x).
Axes of the slice: x: 2, y: 2, z: 4, core: 2. Of those that a mesh axis runs over, the one named last changes fastest.
Arguments:
- distribution: bfloat16 [96, 9, 8, 3072], P('energy', None, 'space'), may hold values from -6 to 6
- region_map: int32 [8, 3072], P('space'), may hold values from 0 to 3
- contact_mask: int32 [8, 3072], P('space'), may hold values 0 or 1
- doping_levels: float32 [4], replicated, may hold values from -2 to 2
- coupling: bfloat16 [2, 3, 9, 9], replicated, may hold values from -1.796875 to 1.796875
- level_coef: float32 [96, 3], P('energy'), may hold values from 0.3 to 1.2
- phonon_kernel: float32 [2, 96, 9], P(None, 'energy'), may hold values from 0.2 to 1
- out_rate: float32 [96, 9], P('energy'), may hold values from 0.5 to 2
Outputs:
- updated: bfloat16 [96, 9, 8, 3072], P('energy', None, 'space')
- potential: float32 [8, 3072], P('space')
The draws below stay inside these ranges and needn't reach their ends.
All inputs are finite; a program needn't handle non-finite values. No bound on the sum of `contact_mask` on one device may be relied on, other than what follows from the above.
Results may differ from the reference program's by a relative error of at most 0.0006.
Values may be sent and summed in bfloat16 or wider, within the bound.
A program may use at most 128 MiB of HBM per device.

```python
import math
import jax
import jax.numpy as jnp
from jax import lax

H = 9
Y = 64
Z = 48
SHIFT = 6
REGIONS = 4
E = 96
X = 8


def set_ends(values, own_key, low, largest):
    index_at = [jax.random.randint(jax.random.fold_in(own_key, axis), (), 0, length) for axis, length in enumerate(values.shape)]
    widest = values.shape.index(max(values.shape))
    next_to = index_at[:widest] + [(index_at[widest] + 1) % values.shape[widest]] + index_at[widest + 1:]
    return values.at[tuple(index_at)].set(low).at[tuple(next_to)].set(largest)


def block_scale(key, shape, shards, smallest, largest):
    def one(position, blocks):
        heights = jax.random.uniform(jax.random.fold_in(jax.random.fold_in(key, 6), position), (blocks,), jnp.float32, smallest / len(shards), largest / len(shards))
        return jnp.repeat(jnp.exp(heights), shape[position] // blocks).reshape((-1,) + (1,) * (len(shape) - position - 1))

    loudness = one(*shards[0])
    for cut in shards[1:]:
        loudness = loudness * one(*cut)
    return loudness


def normal_values(stream_key, extent, deviation, limit, cuts=(), kind=jnp.bfloat16):
    values = jax.random.normal(stream_key, extent, jnp.float32) * deviation
    if len(cuts) > 0:
        values = block_scale(stream_key, extent, cuts, -0.22, 0.18) * values
    return jnp.clip(values, min=-limit, max=limit).astype(kind)


def setup_inputs(seed: int = 0) -> dict:
    key_of = jax.random.split(jax.random.key(seed), 9)
    distribution = normal_values(key_of[0], (E, H, X, Y * Z), 1.0, 6.0, ((0, 16), (2, 2)))
    region_map = set_ends(jax.random.randint(key_of[1], (X, Y * Z), 0, REGIONS), jax.random.fold_in(key_of[1], 1), 0, REGIONS - 1).astype(jnp.int32)
    contact_mask = set_ends((jax.random.randint(key_of[2], (X, Y * Z), 0, 8) < 1).astype(jnp.int32), jax.random.fold_in(key_of[2], 1), 0, 1)
    doping_levels = jnp.clip(jax.random.uniform(key_of[3], (REGIONS,), jnp.float32, -2.0, 2.0), -2.0, 2.0)
    coupling = normal_values(key_of[4], (2, 3, H, H), 0.3, 1.796875)
    level_coef = jnp.clip(0.3 + 0.90000004 * jax.random.uniform(key_of[5], (E, 3), jnp.float32) ** block_scale(key_of[5], (E, 3), ((0, 16),), -0.2, 0.2), 0.3, 1.2)
    phonon_kernel = jnp.clip(jnp.exp(math.log(1.0) - 1.609438 * jax.random.uniform(key_of[6], (2, E, H), jnp.float32) ** block_scale(key_of[6], (2, E, H), ((1, 16),), -0.2, 0.2)), 0.2, 1.0)
    out_rate = jnp.clip(jnp.exp(math.log(2.0) - 1.3862944 * jax.random.uniform(key_of[7], (E, H), jnp.float32) ** block_scale(key_of[7], (E, H), ((0, 16),), -0.2, 0.2)), 0.5, 2.0)
    return dict(distribution=distribution, region_map=region_map, contact_mask=contact_mask, doping_levels=doping_levels, coupling=coupling, level_coef=level_coef, phonon_kernel=phonon_kernel, out_rate=out_rate)


step_time = 0.4
contact_rate = 2.0
highest = lax.Precision.HIGHEST

def sine_table(count):
    indices = jnp.arange(count, dtype=jnp.float32) + 1.0
    angles = math.pi * indices[:, None] * indices[None, :] / (count + 1)
    return math.sqrt(2.0 / (count + 1)) * jnp.sin(angles)

def eigen_row(count):
    indices = jnp.arange(count, dtype=jnp.float32) + 1.0
    return 2.0 - 2.0 * jnp.cos(math.pi * indices / (count + 1))

def back_minus_front(values, dimension):
    length = values.shape[dimension]
    widths = [(0, 0)] * values.ndim
    widths[dimension] = (1, 1)
    padded = jnp.pad(values, widths)
    return 0.5 * (lax.slice_in_dim(padded, 0, length, axis=dimension) - lax.slice_in_dim(padded, 2, length + 2, axis=dimension))

def reference(distribution, region_map, contact_mask, doping_levels, coupling, level_coef, phonon_kernel, out_rate):
    coupling_wide = coupling.astype(jnp.float32)
    isotropic = distribution[:, 0].astype(jnp.float32)
    density = jnp.einsum('e,exc->xc', level_coef[:, 2], isotropic, precision=highest) / math.sqrt(E)
    charge = (density - doping_levels[region_map]).reshape(X, Y, Z)
    table_x = sine_table(X)
    table_y = sine_table(Y)
    table_z = sine_table(Z)
    spectral = jnp.einsum('abc,ai,bj,ck->ijk', charge, table_x, table_y, table_z, precision=highest)
    spectral = spectral / (eigen_row(X)[:, None, None] + eigen_row(Y)[None, :, None] + eigen_row(Z)[None, None, :])
    potential = jnp.einsum('ijk,ai,bj,ck->abc', spectral, table_x, table_y, table_z, precision=highest)
    fields = jnp.stack([back_minus_front(potential, 0), back_minus_front(potential, 1), back_minus_front(potential, 2)]).reshape(3, X, Y * Z)
    contact_term = contact_rate * contact_mask.astype(jnp.float32)

    def one_level(level_index):
        current = distribution[level_index].astype(jnp.float32)
        index_above = jnp.minimum(level_index + SHIFT, E - 1)
        index_below = jnp.maximum(level_index - SHIFT, 0)
        valid_above = (level_index + SHIFT < E).astype(jnp.float32)
        valid_below = (level_index - SHIFT >= 0).astype(jnp.float32)
        from_above = distribution[index_above].astype(jnp.float32) * valid_above
        from_below = distribution[index_below].astype(jnp.float32) * valid_below
        cube_levels = current.reshape(H, X, Y, Z)
        derivs = [-back_minus_front(cube_levels, direction).reshape(H, X, Y * Z) for direction in (1, 2, 3)]
        velocity = level_coef[level_index, 0]
        field_pull = 3.0 * level_coef[level_index, 1]
        change = phonon_kernel[0, level_index][:, None, None] * from_above + phonon_kernel[1, level_index][:, None, None] * from_below
        for direction in range(3):
            change = change - velocity * jnp.einsum('hk,kxc->hxc', coupling_wide[0, direction], derivs[direction], precision=highest)
            change = change + field_pull * fields[direction][None] * jnp.einsum('hk,kxc->hxc', coupling_wide[1, direction], current, precision=highest)
        decay_rate = out_rate[level_index][:, None, None] + contact_term[None]
        return ((current + step_time * change) / (1.0 + step_time * decay_rate)).astype(jnp.bfloat16)
    updated = lax.map(one_level, jnp.arange(E, dtype=jnp.int32))
    return (updated, potential.reshape(X, Y * Z))
```

```python
import functools
import math

import jax
import jax.numpy as jnp
import numpy as np
from jax import lax
from jax.experimental import pallas as pl
from jax.experimental.pallas import tpu as pltpu
from jax.sharding import PartitionSpec as P

Y = 64
Z = 48
step_time = 0.4
contact_rate = 2.0
highest = lax.Precision.HIGHEST
MESH = pl.DeviceIdType.MESH
LANE = 128
GROUP = math.lcm(Z, LANE)
PER = GROUP // Z


def round_up(value, unit):
    return -(-value // unit) * unit


def sine(count):
    index = np.arange(count) + 1.0
    return math.sqrt(2.0 / (count + 1)) * np.sin(math.pi * np.outer(index, index) / (count + 1))


def eigen(count):
    return 2.0 - 2.0 * np.cos(math.pi * (np.arange(count) + 1.0) / (count + 1))


def tables(levels, harmonics, rows, energy, space):
    f32 = np.float32
    count = levels * harmonics * rows
    padded = round_up(count, 16)
    edge_count = levels * harmonics
    edge = round_up(edge_count, 16)
    r = np.arange(count)
    re, rh, rx = r // (harmonics * rows), (r // rows) % harmonics, r % rows
    s = np.arange(edge_count)
    se, sh = s // harmonics, s % harmonics
    pick = np.zeros((padded, LANE), f32)
    pick[r, rh] = 1
    pick_edge = np.zeros((LANE, 2 * edge), f32)
    pick_edge[sh, s] = 1
    pick_edge[sh, edge + s] = 1
    same_level = re[:, None] == re[None, :]
    masks = np.zeros((3, padded, padded), f32)
    ahead = (rx[None, :] == rx[:, None] + 1) * 0.5 - (rx[None, :] == rx[:, None] - 1) * 0.5
    masks[0, :count, :count] = same_level * ahead
    masks[1, :count, :count] = same_level * (rx[:, None] == rx[None, :]) * 0.5
    masks[2, :count, :count] = same_level * (rx[:, None] == rx[None, :])
    mask_edge = np.zeros((padded, 2 * edge), f32)
    mask_edge[:count, :edge_count] = -0.5 * (re[:, None] == se) * (rx[:, None] == 0)
    mask_edge[:count, edge : edge + edge_count] = 0.5 * (re[:, None] == se) * (rx[:, None] == rows - 1)
    choose = np.zeros((2 * edge, padded), f32)
    choose[s, s * rows] = 1
    choose[edge + s, s * rows + rows - 1] = 1
    dense = np.zeros((8, padded), f32)
    for x8 in range(rows):
        dense[x8, :count] = (rh == 0) & (rx == x8)
    eye = np.eye(padded, dtype=f32)

    groups = Y // PER
    block = Y // energy
    piece = round_up(block * rows, 8)
    total = rows * space
    theta = math.pi * (np.arange(Y) + 1.0) / (Y + 1)
    norm = math.sqrt(2.0 / (Y + 1))
    fc = np.zeros((energy * piece, groups * 8))
    fs = np.zeros((energy * piece, groups * 8))
    bc = np.zeros((groups * 8, energy * piece))
    bs = np.zeros((groups * 8, energy * piece))
    cos_in = np.zeros((energy * piece, GROUP))
    sin_in = np.zeros((energy * piece, GROUP))
    inner = np.repeat(np.arange(PER) + 1.0, Z)
    g = np.arange(groups)
    for j in range(Y):
        for x in range(rows):
            at = (j // block) * piece + (j % block) * rows + x
            cos_in[at], sin_in[at] = np.cos(inner * theta[j]), np.sin(inner * theta[j])
            ca, sa = norm * np.cos(PER * g * theta[j]), norm * np.sin(PER * g * theta[j])
            fc[at, g * 8 + x], fs[at, g * 8 + x] = ca, sa
            for copy in range(x, 8, rows):
                bc[g * 8 + copy, at], bs[g * 8 + copy, at] = ca, sa
    fold = np.zeros((GROUP, LANE))
    fold[:, :Z] = np.tile(sine(Z), (PER, 1))
    table = sine(total)
    into = np.zeros((block * total, space * piece))
    back = np.zeros((space, 2 * piece, block * total))
    field = np.zeros((total, total))
    for x in range(total):
        if x > 0:
            field[x] += 0.5 * table[x - 1]
        if x < total - 1:
            field[x] -= 0.5 * table[x + 1]
    lam = np.ones((energy, block * total, LANE))
    for jl in range(block):
        span = slice(jl * total, (jl + 1) * total)
        for sl in range(space):
            for x in range(rows):
                into[span, sl * piece + jl * rows + x] = table[sl * rows + x]
                back[sl, jl * rows + x, span] = table[sl * rows + x]
                back[sl, piece + jl * rows + x, span] = field[sl * rows + x]
        for q in range(energy):
            lam[q, span, :Z] = 1.0 / (
                eigen(total)[:, None] + eigen(Y)[q * block + jl] + eigen(Z)[None, :]
            )
    depth = np.arange(Y * Z) % Z
    zmask = np.zeros((2, 8, Y * Z))
    zmask[0] = depth > 0
    zmask[1] = depth < Z - 1
    values = dict(
        pick=pick, pick_t=pick.T, pick_edge=pick_edge, masks=masks, mask_edge=mask_edge,
        choose=choose, dense=dense, eye=eye, fc=fc, fs=fs, bc=bc, bs=bs, cos_in=cos_in,
        sin_in=sin_in, fold=fold, fold_t=fold.T, into=into, back=back, lam=lam, zmask=zmask,
    )
    values = {name: np.ascontiguousarray(value, f32) for name, value in values.items()}
    for name in ("choose",):
        values[name] = values[name].astype(jnp.bfloat16)
    return values


def dot32(a, b):
    return jnp.dot(a, b, precision=highest, preferred_element_type=jnp.float32)


def dot16(a, b):
    return jnp.dot(a, b, preferred_element_type=jnp.float32)


def kernel(names, energy, space, rows, scale, *refs):
    c = dict(zip(names, refs))
    (state, region, contact, doping, coupling, coef) = refs[len(names) : len(names) + 6]
    out, potential = refs[len(names) + 6 : len(names) + 8]
    (above, below, edge_out, edge_in, mix, mix_edge, total, charge, folded, modes, got1, part,
     got2, answer, got3, field, contact8, ssem, rsem, esend, erecv, s1, r1, s2, r2, s3, r3) = refs[
        len(names) + 8 :
    ]
    padded, cells = above.shape
    edge = edge_in.shape[0] // 2
    piece = modes.shape[1]
    groups = cells // GROUP
    me = lax.axis_index("energy")
    slab = lax.axis_index("space")

    barrier = pltpu.get_barrier_semaphore()

    @pl.loop(1, energy)
    def _(o):
        pl.semaphore_signal(
            barrier, inc=1, device_id={"energy": lax.rem(me + o, energy)}, device_id_type=MESH
        )

    @pl.loop(1, space)
    def _(o):
        pl.semaphore_signal(
            barrier, inc=1, device_id={"space": lax.rem(slab + o, space)}, device_id_type=MESH
        )

    pl.semaphore_wait(barrier, energy + space - 2)

    def lanes(g):
        return pl.ds(pl.multiple_of(g * GROUP, LANE), GROUP)

    def inside(g):
        return pl.ds(pl.multiple_of(g * GROUP + LANE, LANE), GROUP)

    def level_copy(g, up):
        target = jnp.minimum(me + 1, energy - 1) if up else jnp.maximum(me - 1, 0)
        return pltpu.make_async_remote_copy(
            src_ref=state.at[:, inside(g)],
            dst_ref=(below if up else above).at[:, lanes(g)],
            send_sem=ssem.at[int(up), g],
            recv_sem=rsem.at[int(up), g],
            device_id={"energy": target},
            device_id_type=MESH,
        )

    @pl.loop(0, groups)
    def _(g):
        @pl.when(me < energy - 1)
        def _():
            level_copy(g, True).start()

        @pl.when(me > 0)
        def _():
            level_copy(g, False).start()

    weight = dot32(c["dense"][...], coef[:, 2:3] * c["eye"][...]) * scale
    high = weight.astype(jnp.bfloat16)
    rest = weight - high.astype(jnp.float32)
    middle = rest.astype(jnp.bfloat16)
    low = (rest - middle.astype(jnp.float32)).astype(jnp.bfloat16)
    weights = jnp.concatenate([high, middle], axis=0)
    weights_low = jnp.concatenate([low, jnp.zeros_like(low)], axis=0)
    mine = jnp.where(me == 0, 1.0, 0.0).astype(jnp.float32)

    charge[...] = jnp.zeros_like(charge)
    for first in range(0, 8, rows):
        contact8[first : first + rows, :] = contact[...].astype(jnp.float32)
    found = jnp.zeros(region.shape, jnp.float32)
    for kind in range(doping.shape[0]):
        found = found + jnp.where(region[...] == kind, doping[kind], 0.0)
    charge[0:rows, :] = -found * mine
    choose = c["choose"][...]
    for g in range(groups):
        span = slice(g * GROUP, (g + 1) * GROUP)
        block = state[:, g * GROUP + LANE : (g + 1) * GROUP + LANE]
        parts = dot16(weights, block)
        fine = dot16(weights_low, block)
        folded[g * 8 : (g + 1) * 8, :] = parts[0:8] + (parts[8:16] + fine[0:8]) + charge[:, span]
        edge_out[:, span] = dot16(choose, block).astype(jnp.bfloat16)

    def edge_copy(up):
        target = jnp.minimum(slab + 1, space - 1) if up else jnp.maximum(slab - 1, 0)
        src = pl.ds(edge, edge) if up else pl.ds(0, edge)
        dst = pl.ds(0, edge) if up else pl.ds(edge, edge)
        return pltpu.make_async_remote_copy(
            src_ref=edge_out.at[src],
            dst_ref=edge_in.at[dst],
            send_sem=esend.at[int(up)],
            recv_sem=erecv.at[int(up)],
            device_id={"space": target},
            device_id_type=MESH,
        )

    charges = folded[...]
    turned = c["sin_in"][...] * dot32(c["fc"][...], charges) + c["cos_in"][...] * dot32(
        c["fs"][...], charges
    )
    modes[...] = dot32(turned, c["fold"][...]).reshape(modes.shape)

    def spread(source, fixed, got, sends, recvs, o, sending):
        other = lax.rem(me + o, energy) if sending else lax.rem(me + energy - o, energy)
        return pltpu.make_async_remote_copy(
            src_ref=source if fixed else source.at[other],
            dst_ref=got.at[me if sending else other],
            send_sem=sends.at[o],
            recv_sem=recvs.at[me if sending else other],
            device_id={"energy": other},
            device_id_type=MESH,
        )

    @pl.loop(1, energy)
    def _(o):
        spread(modes, False, got1, s1, r1, o, True).start()

    @pl.when(slab < space - 1)
    def _():
        edge_copy(True).start()

    @pl.when(slab > 0)
    def _():
        edge_copy(False).start()

    pick, pick_t = c["pick"][...], c["pick_t"][...]
    for d in range(6):
        wide = dot16(pick, coupling[d])
        mask = c["masks"][0 if d == 0 else 1 if d < 3 else 2]
        mix[d] = (dot16(wide, pick_t) * mask).astype(jnp.bfloat16)
        if d == 0:
            mix_edge[...] = (dot16(wide, c["pick_edge"][...]) * c["mask_edge"][...]).astype(
                jnp.bfloat16
            )

    speed = step_time * coef[:, 0:1]
    pull = (step_time * 3.0) * coef[:, 1:2]
    rate_up = step_time * coef[:, 3:4]
    rate_down = step_time * coef[:, 4:5]
    plain = 1.0 / (1.0 + step_time * coef[:, 5:6])
    held = 1.0 / (1.0 + step_time * (coef[:, 5:6] + contact_rate)) - plain

    @pl.loop(0, groups)
    def _(g):
        block = state[:, inside(g)]
        around = state[:, pl.ds(pl.multiple_of(g * GROUP, LANE), GROUP + 2 * LANE)]
        size = GROUP + 2 * LANE
        ty = dot16(mix[1], around)
        ty = (pltpu.roll(ty, size - Z, axis=1) - pltpu.roll(ty, Z, axis=1))[:, LANE : LANE + GROUP]
        tz = dot16(mix[2], block)
        tz = pltpu.roll(tz, GROUP - 1, axis=1) * c["zmask"][1, 0:1, 0:GROUP] - pltpu.roll(
            tz, 1, axis=1
        ) * c["zmask"][0, 0:1, 0:GROUP]
        total[:, lanes(g)] = block.astype(jnp.float32) - speed * (dot16(mix[0], block) + ty + tz)

    @pl.loop(1, energy)
    def _(o):
        spread(modes, False, got1, s1, r1, o, False).wait_recv()

    got1[me] = modes[me]
    summed = got1[0]
    for q in range(1, energy):
        summed = summed + got1[q]
    part[...] = summed

    def pencil(o, sending):
        other = lax.rem(slab + o, space) if sending else lax.rem(slab + space - o, space)
        return pltpu.make_async_remote_copy(
            src_ref=part,
            dst_ref=got2.at[slab if sending else other],
            send_sem=s2.at[o],
            recv_sem=r2.at[slab if sending else other],
            device_id={"space": other},
            device_id_type=MESH,
        )

    @pl.loop(1, space)
    def _(o):
        pencil(o, True).start()

    got2[slab] = part[...]

    @pl.loop(1, space)
    def _(o):
        pencil(o, False).wait_recv()

    spectral = dot32(c["into"][...], got2[...].reshape(space * piece, LANE)) * c["lam"][me]
    answer[...] = dot32(c["back"][slab], spectral)

    @pl.loop(1, energy)
    def _(o):
        spread(answer, True, got3, s3, r3, o, True).start()

    got3[me] = answer[...]

    @pl.loop(1, energy)
    def _(o):
        spread(answer, True, got3, s3, r3, o, False).wait_recv()

    for which in range(2):
        lines = got3[:, which * piece : (which + 1) * piece, :].reshape(energy * piece, LANE)
        lines = dot32(lines, c["fold_t"][...])
        lines = dot32(c["bs"][...], c["cos_in"][...] * lines) + dot32(
            c["bc"][...], c["sin_in"][...] * lines
        )
        for g in range(groups):
            span = slice(g * GROUP, (g + 1) * GROUP)
            if which == 0:
                charge[:, span] = lines[g * 8 : (g + 1) * 8]
            else:
                field[0, :, span] = lines[g * 8 : (g + 1) * 8]
    level = charge[...]
    potential[...] = level[0:rows]
    column = lax.broadcasted_iota(jnp.int32, level.shape, 1)
    field[1] = 0.5 * (
        jnp.where(column >= Z, pltpu.roll(level, Z, axis=1), 0.0)
        - jnp.where(column < cells - Z, pltpu.roll(level, cells - Z, axis=1), 0.0)
    )
    field[2] = 0.5 * (
        c["zmask"][0] * pltpu.roll(level, 1, axis=1)
        - c["zmask"][1] * pltpu.roll(level, cells - 1, axis=1)
    )

    @pl.when(slab > 0)
    def _():
        edge_copy(True).wait_recv()

    @pl.when(slab == 0)
    def _():
        edge_in[0:edge, :] = jnp.zeros((edge, cells), jnp.bfloat16)

    @pl.when(slab < space - 1)
    def _():
        edge_copy(False).wait_recv()

    @pl.when(slab == space - 1)
    def _():
        edge_in[edge : 2 * edge, :] = jnp.zeros((edge, cells), jnp.bfloat16)

    @pl.when(me == 0)
    def _():
        below[...] = jnp.zeros_like(below)

    @pl.when(me == energy - 1)
    def _():
        above[...] = jnp.zeros_like(above)

    def over(values):
        return values.reshape(padded // 8, 8, GROUP)

    @pl.loop(0, groups)
    def _(g):
        block = state[:, inside(g)]
        pulled = over(dot16(mix[3], block)) * field[0, :, lanes(g)][None]
        pulled = pulled + over(dot16(mix[4], block)) * field[1, :, lanes(g)][None]
        pulled = pulled + over(dot16(mix[5], block)) * field[2, :, lanes(g)][None]
        total[:, lanes(g)] = (
            total[:, lanes(g)]
            + pull * pulled.reshape(padded, GROUP)
            - speed * dot16(mix_edge[...], edge_in[:, lanes(g)])
        )

    @pl.loop(0, groups)
    def _(g):
        @pl.when(me > 0)
        def _():
            level_copy(g, True).wait_recv()

        @pl.when(me < energy - 1)
        def _():
            level_copy(g, False).wait_recv()

        value = (
            total[:, lanes(g)]
            + rate_up * above[:, lanes(g)].astype(jnp.float32)
            + rate_down * below[:, lanes(g)].astype(jnp.float32)
        )
        spots = jnp.broadcast_to(
            contact8[:, lanes(g)][None], (padded // 8, 8, GROUP)
        ).reshape(padded, GROUP)
        out[:, lanes(g)] = (value * (plain + held * spots)).astype(jnp.bfloat16)

    @pl.loop(0, groups)
    def _(g):
        @pl.when(me < energy - 1)
        def _():
            level_copy(g, True).wait_send()

        @pl.when(me > 0)
        def _():
            level_copy(g, False).wait_send()

    @pl.loop(1, energy)
    def _(o):
        spread(modes, False, got1, s1, r1, o, True).wait_send()
        spread(answer, True, got3, s3, r3, o, True).wait_send()

    @pl.loop(1, space)
    def _(o):
        pencil(o, True).wait_send()

    @pl.when(slab < space - 1)
    def _():
        edge_copy(True).wait_send()

    @pl.when(slab > 0)
    def _():
        edge_copy(False).wait_send()


def local(
    energy,
    space,
    distribution,
    region_map,
    contact_mask,
    doping_levels,
    coupling,
    level_coef,
    phonon_kernel,
    out_rate,
):
    levels, harmonics, rows, cells = distribution.shape
    count = levels * harmonics * rows
    padded = round_up(count, 16)
    edge = round_up(levels * harmonics, 16)
    constants = tables(levels, harmonics, rows, energy, space)
    names = tuple(constants)
    piece = round_up(Y // energy * rows, 8)
    groups = cells // GROUP
    state = jnp.pad(
        distribution.reshape(count, cells), ((0, padded - count), (LANE, LANE))
    )
    shape = (levels, harmonics, rows)
    coef = jnp.stack(
        [jnp.broadcast_to(level_coef[:, i][:, None, None], shape) for i in range(3)]
        + [jnp.broadcast_to(phonon_kernel[i][:, :, None], shape) for i in range(2)]
        + [jnp.broadcast_to(out_rate[:, :, None], shape)],
        axis=-1,
    ).reshape(count, 6)
    coef = jnp.pad(coef, ((0, padded - count), (0, 2)))
    wide = jnp.pad(
        coupling.reshape(6, harmonics, harmonics).astype(jnp.float32),
        ((0, 0), (0, LANE - harmonics), (0, LANE - harmonics)),
    )
    vmem = pl.BlockSpec(memory_space=pltpu.VMEM)
    smem = pl.BlockSpec(memory_space=pltpu.SMEM)
    bf16, f32 = jnp.bfloat16, jnp.float32
    dma = pltpu.SemaphoreType.DMA
    out, potential = pl.pallas_call(
        functools.partial(
            kernel, names, energy, space, rows, 1.0 / math.sqrt(levels * energy)
        ),
        out_shape=(
            jax.ShapeDtypeStruct((padded, cells), bf16),
            jax.ShapeDtypeStruct((rows, cells), f32),
        ),
        in_specs=[vmem] * (len(names) + 3) + [smem] + [vmem] * 2,
        out_specs=(vmem, vmem),
        scratch_shapes=[
            pltpu.VMEM((padded, cells), bf16),
            pltpu.VMEM((padded, cells), bf16),
            pltpu.VMEM((2 * edge, cells), bf16),
            pltpu.VMEM((2 * edge, cells), bf16),
            pltpu.VMEM((6, padded, padded), bf16),
            pltpu.VMEM((padded, 2 * edge), bf16),
            pltpu.VMEM((padded, cells), f32),
            pltpu.VMEM((8, cells), f32),
            pltpu.VMEM((groups * 8, GROUP), f32),
            pltpu.VMEM((energy, piece, LANE), f32),
            pltpu.VMEM((energy, piece, LANE), f32),
            pltpu.VMEM((piece, LANE), f32),
            pltpu.VMEM((space, piece, LANE), f32),
            pltpu.VMEM((2 * piece, LANE), f32),
            pltpu.VMEM((energy, 2 * piece, LANE), f32),
            pltpu.VMEM((3, 8, cells), f32),
            pltpu.VMEM((8, cells), f32),
            dma((2, groups)),
            dma((2, groups)),
            dma((2,)),
            dma((2,)),
            dma((energy,)),
            dma((energy,)),
            dma((space,)),
            dma((space,)),
            dma((energy,)),
            dma((energy,)),
        ],
        compiler_params=pltpu.CompilerParams(
            collective_id=0, has_side_effects=True, vmem_limit_bytes=48 * 1024 * 1024
        ),
        cost_estimate=pl.CostEstimate(
            flops=2 * 7 * padded * padded * cells,
            bytes_accessed=8 * padded * cells,
            transcendentals=0,
        ),
    )(
        *[jnp.asarray(constants[name]) for name in names],
        state,
        region_map,
        contact_mask,
        doping_levels,
        wide,
        coef,
    )
    return out[:count].reshape(distribution.shape), potential


def solution(mesh):
    return jax.shard_map(
        functools.partial(local, mesh.shape["energy"], mesh.shape["space"]),
        mesh=mesh,
        in_specs=(
            P("energy", None, "space", None),
            P("space", None),
            P("space", None),
            P(),
            P(),
            P("energy", None),
            P(None, "energy", None),
            P("energy", None),
        ),
        out_specs=(P("energy", None, "space", None), P("space", None)),
        check_vma=False,
    )
```

```python
import functools
import math

import jax
import jax.numpy as jnp
import numpy as np
from jax import lax
from jax.experimental import pallas as pl
from jax.experimental.pallas import tpu as pltpu
from jax.sharding import PartitionSpec as P

Y = 64
Z = 48
step_time = 0.4
contact_rate = 2.0
highest = lax.Precision.HIGHEST
MESH = pl.DeviceIdType.MESH
LANE = 128
GROUP = math.lcm(Z, LANE)
PER = GROUP // Z


def round_up(value, unit):
    return -(-value // unit) * unit


def sine(count):
    index = np.arange(count) + 1.0
    return math.sqrt(2.0 / (count + 1)) * np.sin(math.pi * np.outer(index, index) / (count + 1))


def eigen(count):
    return 2.0 - 2.0 * np.cos(math.pi * (np.arange(count) + 1.0) / (count + 1))


def tables(levels, harmonics, rows, energy, space):
    f32 = np.float32
    count = levels * harmonics * rows
    padded = round_up(count, 16)
    edge_count = levels * harmonics
    edge = round_up(edge_count, 16)
    r = np.arange(count)
    re, rh, rx = r // (harmonics * rows), (r // rows) % harmonics, r % rows
    s = np.arange(edge_count)
    se, sh = s // harmonics, s % harmonics
    pick = np.zeros((padded, harmonics), f32)
    pick[r, rh] = 1
    pick_level = np.zeros((padded, levels), f32)
    pick_level[r, re] = 1
    pick_edge = np.zeros((harmonics, 2 * edge), f32)
    pick_edge[sh, s] = 1
    pick_edge[sh, edge + s] = 1
    same_level = re[:, None] == re[None, :]
    masks = np.zeros((3, padded, padded), f32)
    ahead = (rx[None, :] == rx[:, None] + 1) * 0.5 - (rx[None, :] == rx[:, None] - 1) * 0.5
    masks[0, :count, :count] = same_level * ahead
    masks[1, :count, :count] = same_level * (rx[:, None] == rx[None, :]) * 0.5
    masks[2, :count, :count] = same_level * (rx[:, None] == rx[None, :])
    mask_edge = np.zeros((padded, 2 * edge), f32)
    mask_edge[:count, :edge_count] = -0.5 * (re[:, None] == se) * (rx[:, None] == 0)
    mask_edge[:count, edge : edge + edge_count] = 0.5 * (re[:, None] == se) * (rx[:, None] == rows - 1)
    choose = np.zeros((2 * edge, padded), f32)
    choose[s, s * rows] = 1
    choose[edge + s, s * rows + rows - 1] = 1
    dense = np.zeros((8, padded), f32)
    for x8 in range(rows):
        dense[x8, :count] = (rh == 0) & (rx == x8)

    groups = Y // PER
    block = Y // energy
    piece = round_up(block * rows, 8)
    total = rows * space
    theta = math.pi * (np.arange(Y) + 1.0) / (Y + 1)
    norm = math.sqrt(2.0 / (Y + 1))
    fc = np.zeros((energy * piece, groups * 8))
    fs = np.zeros((energy * piece, groups * 8))
    bc = np.zeros((groups * 8, energy * piece))
    bs = np.zeros((groups * 8, energy * piece))
    cos_in = np.zeros((energy * piece, GROUP))
    sin_in = np.zeros((energy * piece, GROUP))
    inner = np.repeat(np.arange(PER) + 1.0, Z)
    g = np.arange(groups)
    for j in range(Y):
        for x in range(rows):
            at = (j // block) * piece + (j % block) * rows + x
            cos_in[at], sin_in[at] = np.cos(inner * theta[j]), np.sin(inner * theta[j])
            ca, sa = norm * np.cos(PER * g * theta[j]), norm * np.sin(PER * g * theta[j])
            fc[at, g * 8 + x], fs[at, g * 8 + x] = ca, sa
            for copy in range(x, 8, rows):
                bc[g * 8 + copy, at], bs[g * 8 + copy, at] = ca, sa
    fold = np.zeros((GROUP, LANE))
    half = LANE // 2
    fold[:, :Z] = np.tile(sine(Z), (PER, 1))
    fold[:, half : half + Z] = fold[:, :Z]
    unfold = np.zeros((2, LANE, GROUP))
    unfold[0, :Z] = fold[:, :Z].T
    unfold[1, half : half + Z] = fold[:, :Z].T
    table = sine(total)
    into = np.zeros((block * total, space * piece))
    back = np.zeros((space, 2 * piece, block * total))
    field = np.zeros((total, total))
    for x in range(total):
        if x > 0:
            field[x] += 0.5 * table[x - 1]
        if x < total - 1:
            field[x] -= 0.5 * table[x + 1]
    lam = np.ones((energy, block * total, LANE))
    for jl in range(block):
        span = slice(jl * total, (jl + 1) * total)
        for sl in range(space):
            for x in range(rows):
                into[span, sl * piece + jl * rows + x] = table[sl * rows + x]
                back[sl, jl * rows + x, span] = table[sl * rows + x]
                back[sl, piece + jl * rows + x, span] = field[sl * rows + x]
        for q in range(energy):
            lam[q, span, :Z] = 1.0 / (
                eigen(total)[:, None] + eigen(Y)[q * block + jl] + eigen(Z)[None, :]
            )
            lam[q, span, half : half + Z] = lam[q, span, :Z]
    depth = np.arange(Y * Z) % Z
    zmask = np.zeros((2, 8, Y * Z))
    zmask[0] = depth > 0
    zmask[1] = depth < Z - 1
    values = dict(
        pick=pick, pick_t=pick.T, pick_edge=pick_edge, masks=masks, mask_edge=mask_edge,
        choose=choose, dense=dense, pick_level=pick_level,
        pick_level_t=pick_level.T, fc=fc, fs=fs, bc=bc, bs=bs, cos_in=cos_in,
        sin_in=sin_in, fold=fold, unfold=unfold, into=into, back=back, lam=lam, zmask=zmask,
    )
    values = {name: np.ascontiguousarray(value, f32) for name, value in values.items()}
    for name in ("choose", "masks", "mask_edge"):
        values[name] = values[name].astype(jnp.bfloat16)
    return values


def dot32(a, b):
    return jnp.dot(a, b, precision=highest, preferred_element_type=jnp.float32)


def dot16(a, b):
    return jnp.dot(a, b, preferred_element_type=jnp.float32)


def kernel(names, energy, space, rows, scale, *refs):
    c = dict(zip(names, refs))
    (given, region, contact, doping, coupling, level_coef, level_coef_t, phonon, out_rate) = refs[
        len(names) : len(names) + 9
    ]
    out, potential = refs[len(names) + 9 : len(names) + 11]
    (state, above, below, edge_out, edge_in, mix, mix_edge, total, pulls, charge, folded, modes, got1, part,
     got2, answer, got3, field, contact8, ssem, rsem, esend, erecv, s1, r1, s2, r2, s3, r3) = refs[
        len(names) + 11 :
    ]
    padded, cells = above.shape
    edge = edge_in.shape[0] // 2
    piece = modes.shape[1]
    groups = cells // GROUP
    me = lax.axis_index("energy")
    slab = lax.axis_index("space")

    barrier = pltpu.get_barrier_semaphore()

    @pl.loop(1, energy)
    def _(o):
        pl.semaphore_signal(
            barrier, inc=1, device_id={"energy": lax.rem(me + o, energy)}, device_id_type=MESH
        )

    @pl.loop(1, space)
    def _(o):
        pl.semaphore_signal(
            barrier, inc=1, device_id={"space": lax.rem(slab + o, space)}, device_id_type=MESH
        )

    pl.semaphore_wait(barrier, energy + space - 2)

    def lanes(g):
        return pl.ds(pl.multiple_of(g * GROUP, LANE), GROUP)

    def inside(g):
        return pl.ds(pl.multiple_of(g * GROUP + LANE, LANE), GROUP)

    def level_copy(g, up):
        target = jnp.minimum(me + 1, energy - 1) if up else jnp.maximum(me - 1, 0)
        return pltpu.make_async_remote_copy(
            src_ref=state.at[:, inside(g)],
            dst_ref=(below if up else above).at[:, lanes(g)],
            send_sem=ssem.at[int(up), g],
            recv_sem=rsem.at[int(up), g],
            device_id={"energy": target},
            device_id_type=MESH,
        )

    def send_levels(first, last):
        @pl.loop(first, last)
        def _(g):
            @pl.when(me < energy - 1)
            def _():
                level_copy(g, True).start()

            @pl.when(me > 0)
            def _():
                level_copy(g, False).start()

    state[:, 0:LANE] = jnp.zeros((padded, LANE), jnp.bfloat16)
    state[:, cells + LANE :] = jnp.zeros((padded, LANE), jnp.bfloat16)
    count = given.shape[0] * rows

    @pl.loop(0, groups)
    def _(g):
        block = given[:, :, lanes(g)].astype(jnp.float32).reshape(count, GROUP)
        block = jnp.concatenate([block, jnp.zeros((padded - count, GROUP), jnp.float32)], axis=0)
        state[:, inside(g)] = block.astype(jnp.bfloat16)

    first, second, third = groups // 4, groups // 2, groups * 5 // 8
    send_levels(0, first)

    density = dot32(level_coef_t[...], c["pick_level_t"][...])[2:3, :]
    weight = c["dense"][...] * density * scale
    high = weight.astype(jnp.bfloat16)
    rest = weight - high.astype(jnp.float32)
    middle = rest.astype(jnp.bfloat16)
    low = (rest - middle.astype(jnp.float32)).astype(jnp.bfloat16)
    weights = jnp.concatenate([high, middle], axis=0)
    weights_low = jnp.concatenate([low, jnp.zeros_like(low)], axis=0)
    mine = jnp.where(me == 0, 1.0, 0.0).astype(jnp.float32)

    charge[...] = jnp.zeros_like(charge)
    for row in range(0, 8, rows):
        contact8[row : row + rows, :] = contact[...].astype(jnp.float32)
    found = jnp.zeros(region.shape, jnp.float32)
    for kind in range(doping.shape[0]):
        found = found + jnp.where(region[...] == kind, doping[kind], 0.0)
    charge[0:rows, :] = -found * mine
    choose = c["choose"][...]
    for g in range(groups):
        span = slice(g * GROUP, (g + 1) * GROUP)
        block = state[:, g * GROUP + LANE : (g + 1) * GROUP + LANE]
        parts = dot16(weights, block)
        fine = dot16(weights_low, block)
        folded[g * 8 : (g + 1) * 8, :] = parts[0:8] + (parts[8:16] + fine[0:8]) + charge[:, span]
        edge_out[:, span] = dot16(choose, block).astype(jnp.bfloat16)

    def edge_copy(up):
        target = jnp.minimum(slab + 1, space - 1) if up else jnp.maximum(slab - 1, 0)
        src = pl.ds(edge, edge) if up else pl.ds(0, edge)
        dst = pl.ds(0, edge) if up else pl.ds(edge, edge)
        return pltpu.make_async_remote_copy(
            src_ref=edge_out.at[src],
            dst_ref=edge_in.at[dst],
            send_sem=esend.at[int(up)],
            recv_sem=erecv.at[int(up)],
            device_id={"space": target},
            device_id_type=MESH,
        )

    charges = folded[...]
    turned = c["sin_in"][...] * dot32(c["fc"][...], charges) + c["cos_in"][...] * dot32(
        c["fs"][...], charges
    )
    modes[...] = dot32(turned, c["fold"][...]).reshape(modes.shape)

    def spread(source, fixed, got, sends, recvs, o, sending):
        other = lax.rem(me + o, energy) if sending else lax.rem(me + energy - o, energy)
        return pltpu.make_async_remote_copy(
            src_ref=source if fixed else source.at[other],
            dst_ref=got.at[me if sending else other],
            send_sem=sends.at[o],
            recv_sem=recvs.at[me if sending else other],
            device_id={"energy": other},
            device_id_type=MESH,
        )

    @pl.loop(1, energy)
    def _(o):
        spread(modes, False, got1, s1, r1, o, True).start()

    send_levels(first, second)

    pick, pick_t = c["pick"][...], c["pick_t"][...]
    for d in range(6):
        wide = dot16(pick, coupling[d // 3, d % 3].astype(jnp.float32))
        mask = c["masks"][0 if d == 0 else 1 if d < 3 else 2].astype(jnp.float32)
        mix[d] = (dot16(wide, pick_t) * mask).astype(jnp.bfloat16)
        if d == 0:
            mix_edge[...] = (dot16(wide, c["pick_edge"][...]) * c["mask_edge"][...]).astype(
                jnp.bfloat16
            )

    def by_row(values):
        return jnp.sum(dot32(c["pick_level"][...], values) * pick, axis=1, keepdims=True)

    coef = dot32(c["pick_level"][...], level_coef[...])
    speed = step_time * coef[:, 0:1]
    pull = (step_time * 3.0) * coef[:, 1:2]
    rate_up = step_time * by_row(phonon[0])
    rate_down = step_time * by_row(phonon[1])
    decay = by_row(out_rate[...])
    plain = 1.0 / (1.0 + step_time * decay)
    held = 1.0 / (1.0 + step_time * (decay + contact_rate)) - plain

    @pl.loop(0, groups)
    def _(g):
        block = state[:, inside(g)]
        around = state[:, pl.ds(pl.multiple_of(g * GROUP, LANE), GROUP + 2 * LANE)]
        size = GROUP + 2 * LANE
        ty = dot16(mix[1], around)
        ty = (pltpu.roll(ty, size - Z, axis=1) - pltpu.roll(ty, Z, axis=1))[:, LANE : LANE + GROUP]
        tz = dot16(mix[2], block)
        tz = pltpu.roll(tz, GROUP - 1, axis=1) * c["zmask"][1, 0:1, 0:GROUP] - pltpu.roll(
            tz, 1, axis=1
        ) * c["zmask"][0, 0:1, 0:GROUP]
        total[:, lanes(g)] = block.astype(jnp.float32) - speed * (dot16(mix[0], block) + ty + tz)
        for d in range(3):
            pulls[d, :, lanes(g)] = dot16(mix[3 + d], block)

    @pl.loop(1, energy)
    def _(o):
        spread(modes, False, got1, s1, r1, o, False).wait_recv()

    got1[me] = modes[me]
    summed = got1[0]
    for q in range(1, energy):
        summed = summed + got1[q]
    part[...] = summed

    def pencil(o, sending):
        other = lax.rem(slab + o, space) if sending else lax.rem(slab + space - o, space)
        return pltpu.make_async_remote_copy(
            src_ref=part,
            dst_ref=got2.at[slab if sending else other],
            send_sem=s2.at[o],
            recv_sem=r2.at[slab if sending else other],
            device_id={"space": other},
            device_id_type=MESH,
        )

    @pl.loop(1, space)
    def _(o):
        pencil(o, True).start()

    send_levels(second, third)

    @pl.when(slab < space - 1)
    def _():
        edge_copy(True).start()

    @pl.when(slab > 0)
    def _():
        edge_copy(False).start()

    got2[slab] = part[...]

    @pl.loop(1, space)
    def _(o):
        pencil(o, False).wait_recv()

    spectral = dot32(c["into"][...], got2[...].reshape(space * piece, LANE)) * c["lam"][me]
    both = dot32(c["back"][slab], spectral)
    lower = lax.broadcasted_iota(jnp.int32, (piece, LANE), 1) < LANE // 2
    answer[...] = jnp.where(lower, both[0:piece], both[piece:])

    @pl.loop(1, energy)
    def _(o):
        spread(answer, True, got3, s3, r3, o, True).start()

    send_levels(third, groups)
    got3[me] = answer[...]

    @pl.loop(1, energy)
    def _(o):
        spread(answer, True, got3, s3, r3, o, False).wait_recv()

    for which in range(2):
        lines = dot32(got3[...].reshape(energy * piece, LANE), c["unfold"][which])
        lines = dot32(c["bs"][...], c["cos_in"][...] * lines) + dot32(
            c["bc"][...], c["sin_in"][...] * lines
        )
        for g in range(groups):
            span = slice(g * GROUP, (g + 1) * GROUP)
            if which == 0:
                charge[:, span] = lines[g * 8 : (g + 1) * 8]
            else:
                field[0, :, span] = lines[g * 8 : (g + 1) * 8]
    level = charge[...]
    potential[...] = level[0:rows]
    column = lax.broadcasted_iota(jnp.int32, level.shape, 1)
    field[1] = 0.5 * (
        jnp.where(column >= Z, pltpu.roll(level, Z, axis=1), 0.0)
        - jnp.where(column < cells - Z, pltpu.roll(level, cells - Z, axis=1), 0.0)
    )
    field[2] = 0.5 * (
        c["zmask"][0] * pltpu.roll(level, 1, axis=1)
        - c["zmask"][1] * pltpu.roll(level, cells - 1, axis=1)
    )

    @pl.when(slab > 0)
    def _():
        edge_copy(True).wait_recv()

    @pl.when(slab == 0)
    def _():
        edge_in[0:edge, :] = jnp.zeros((edge, cells), jnp.bfloat16)

    @pl.when(slab < space - 1)
    def _():
        edge_copy(False).wait_recv()

    @pl.when(slab == space - 1)
    def _():
        edge_in[edge : 2 * edge, :] = jnp.zeros((edge, cells), jnp.bfloat16)

    @pl.when(me == 0)
    def _():
        below[...] = jnp.zeros_like(below)

    @pl.when(me == energy - 1)
    def _():
        above[...] = jnp.zeros_like(above)

    def over(values):
        return values.reshape(padded // 8, 8, GROUP)

    @pl.loop(0, groups)
    def _(g):
        pulled = over(pulls[0, :, lanes(g)]) * field[0, :, lanes(g)][None]
        pulled = pulled + over(pulls[1, :, lanes(g)]) * field[1, :, lanes(g)][None]
        pulled = pulled + over(pulls[2, :, lanes(g)]) * field[2, :, lanes(g)][None]
        total[:, lanes(g)] = (
            total[:, lanes(g)]
            + pull * pulled.reshape(padded, GROUP)
            - speed * dot16(mix_edge[...], edge_in[:, lanes(g)])
        )

    @pl.loop(0, groups)
    def _(g):
        @pl.when(me > 0)
        def _():
            level_copy(g, True).wait_recv()

        @pl.when(me < energy - 1)
        def _():
            level_copy(g, False).wait_recv()

        value = (
            total[:, lanes(g)]
            + rate_up * above[:, lanes(g)].astype(jnp.float32)
            + rate_down * below[:, lanes(g)].astype(jnp.float32)
        )
        spots = jnp.broadcast_to(
            contact8[:, lanes(g)][None], (padded // 8, 8, GROUP)
        ).reshape(padded, GROUP)
        value = (value * (plain + held * spots))[0:count]
        out[:, :, lanes(g)] = value.reshape(count // rows, rows, GROUP).astype(jnp.bfloat16)

    @pl.loop(0, groups)
    def _(g):
        @pl.when(me < energy - 1)
        def _():
            level_copy(g, True).wait_send()

        @pl.when(me > 0)
        def _():
            level_copy(g, False).wait_send()

    @pl.loop(1, energy)
    def _(o):
        spread(modes, False, got1, s1, r1, o, True).wait_send()
        spread(answer, True, got3, s3, r3, o, True).wait_send()

    @pl.loop(1, space)
    def _(o):
        pencil(o, True).wait_send()

    @pl.when(slab < space - 1)
    def _():
        edge_copy(True).wait_send()

    @pl.when(slab > 0)
    def _():
        edge_copy(False).wait_send()


def local(
    energy,
    space,
    distribution,
    region_map,
    contact_mask,
    doping_levels,
    coupling,
    level_coef,
    phonon_kernel,
    out_rate,
):
    levels, harmonics, rows, cells = distribution.shape
    count = levels * harmonics * rows
    padded = round_up(count, 16)
    edge = round_up(levels * harmonics, 16)
    constants = tables(levels, harmonics, rows, energy, space)
    names = tuple(constants)
    piece = round_up(Y // energy * rows, 8)
    groups = cells // GROUP
    vmem = pl.BlockSpec(memory_space=pltpu.VMEM)
    smem = pl.BlockSpec(memory_space=pltpu.SMEM)
    bf16, f32 = jnp.bfloat16, jnp.float32
    dma = pltpu.SemaphoreType.DMA
    out, potential = pl.pallas_call(
        functools.partial(
            kernel, names, energy, space, rows, 1.0 / math.sqrt(levels * energy)
        ),
        out_shape=(
            jax.ShapeDtypeStruct((levels * harmonics, rows, cells), bf16),
            jax.ShapeDtypeStruct((rows, cells), f32),
        ),
        in_specs=[vmem] * (len(names) + 3) + [smem] + [vmem] * 5,
        out_specs=(vmem, vmem),
        scratch_shapes=[
            pltpu.VMEM((padded, cells + 2 * LANE), bf16),
            pltpu.VMEM((padded, cells), bf16),
            pltpu.VMEM((padded, cells), bf16),
            pltpu.VMEM((2 * edge, cells), bf16),
            pltpu.VMEM((2 * edge, cells), bf16),
            pltpu.VMEM((6, padded, padded), bf16),
            pltpu.VMEM((padded, 2 * edge), bf16),
            pltpu.VMEM((padded, cells), f32),
            pltpu.VMEM((3, padded, cells), f32),
            pltpu.VMEM((8, cells), f32),
            pltpu.VMEM((groups * 8, GROUP), f32),
            pltpu.VMEM((energy, piece, LANE), f32),
            pltpu.VMEM((energy, piece, LANE), f32),
            pltpu.VMEM((piece, LANE), f32),
            pltpu.VMEM((space, piece, LANE), f32),
            pltpu.VMEM((piece, LANE), f32),
            pltpu.VMEM((energy, piece, LANE), f32),
            pltpu.VMEM((3, 8, cells), f32),
            pltpu.VMEM((8, cells), f32),
            dma((2, groups)),
            dma((2, groups)),
            dma((2,)),
            dma((2,)),
            dma((energy,)),
            dma((energy,)),
            dma((space,)),
            dma((space,)),
            dma((energy,)),
            dma((energy,)),
        ],
        compiler_params=pltpu.CompilerParams(
            collective_id=0, has_side_effects=True, vmem_limit_bytes=48 * 1024 * 1024
        ),
        cost_estimate=pl.CostEstimate(
            flops=2 * 7 * padded * padded * cells,
            bytes_accessed=8 * padded * cells,
            transcendentals=0,
        ),
    )(
        *[jnp.asarray(constants[name]) for name in names],
        distribution.reshape(levels * harmonics, rows, cells),
        region_map,
        contact_mask,
        doping_levels,
        coupling,
        level_coef,
        level_coef.T,
        phonon_kernel,
        out_rate,
    )
    return out.reshape(distribution.shape), potential


def solution(mesh):
    return jax.shard_map(
        functools.partial(local, mesh.shape["energy"], mesh.shape["space"]),
        mesh=mesh,
        in_specs=(
            P("energy", None, "space", None),
            P("space", None),
            P("space", None),
            P(),
            P(),
            P("energy", None),
            P(None, "energy", None),
            P("energy", None),
        ),
        out_specs=(P("energy", None, "space", None), P("space", None)),
        check_vma=False,
    )
```

```python
import functools
import math

import jax
import jax.numpy as jnp
import numpy as np
from jax import lax
from jax.experimental import pallas as pl
from jax.experimental.pallas import tpu as pltpu
from jax.sharding import PartitionSpec as P

Y = 64
Z = 48
step_time = 0.4
contact_rate = 2.0
highest = lax.Precision.HIGHEST
MESH = pl.DeviceIdType.MESH
LANE = 128
GROUP = math.lcm(Z, LANE)
PER = GROUP // Z


def round_up(value, unit):
    return -(-value // unit) * unit


def sine(count):
    index = np.arange(count) + 1.0
    return math.sqrt(2.0 / (count + 1)) * np.sin(math.pi * np.outer(index, index) / (count + 1))


def eigen(count):
    return 2.0 - 2.0 * np.cos(math.pi * (np.arange(count) + 1.0) / (count + 1))


def tables(levels, harmonics, rows, energy, space):
    f32 = np.float32
    count = levels * harmonics * rows
    padded = round_up(count, 16)
    edge_count = levels * harmonics
    edge = round_up(edge_count, 16)
    r = np.arange(count)
    re, rh, rx = r // (harmonics * rows), (r // rows) % harmonics, r % rows
    s = np.arange(edge_count)
    se, sh = s // harmonics, s % harmonics
    pick = np.zeros((padded, harmonics), f32)
    pick[r, rh] = 1
    pick_level = np.zeros((padded, levels), f32)
    pick_level[r, re] = 1
    pick_edge = np.zeros((harmonics, 2 * edge), f32)
    pick_edge[sh, s] = 1
    pick_edge[sh, edge + s] = 1
    same_level = re[:, None] == re[None, :]
    masks = np.zeros((3, padded, padded), f32)
    ahead = (rx[None, :] == rx[:, None] + 1) * 0.5 - (rx[None, :] == rx[:, None] - 1) * 0.5
    masks[0, :count, :count] = same_level * ahead
    masks[1, :count, :count] = same_level * (rx[:, None] == rx[None, :]) * 0.5
    masks[2, :count, :count] = same_level * (rx[:, None] == rx[None, :])
    mask_edge = np.zeros((padded, 2 * edge), f32)
    mask_edge[:count, :edge_count] = -0.5 * (re[:, None] == se) * (rx[:, None] == 0)
    mask_edge[:count, edge : edge + edge_count] = 0.5 * (re[:, None] == se) * (rx[:, None] == rows - 1)
    choose = np.zeros((2 * edge, padded), f32)
    choose[s, s * rows] = 1
    choose[edge + s, s * rows + rows - 1] = 1
    dense = np.zeros((8, padded), f32)
    for x8 in range(rows):
        dense[x8, :count] = (rh == 0) & (rx == x8)

    groups = Y // PER
    block = Y // energy
    piece = round_up(block * rows, 8)
    total = rows * space
    theta = math.pi * (np.arange(Y) + 1.0) / (Y + 1)
    norm = math.sqrt(2.0 / (Y + 1))
    fc = np.zeros((energy * piece, groups * 8))
    fs = np.zeros((energy * piece, groups * 8))
    bc = np.zeros((groups * 8, energy * piece))
    bs = np.zeros((groups * 8, energy * piece))
    cos_in = np.zeros((energy * piece, GROUP))
    sin_in = np.zeros((energy * piece, GROUP))
    inner = np.repeat(np.arange(PER) + 1.0, Z)
    g = np.arange(groups)
    for j in range(Y):
        for x in range(rows):
            at = (j // block) * piece + (j % block) * rows + x
            cos_in[at], sin_in[at] = np.cos(inner * theta[j]), np.sin(inner * theta[j])
            ca, sa = norm * np.cos(PER * g * theta[j]), norm * np.sin(PER * g * theta[j])
            fc[at, g * 8 + x], fs[at, g * 8 + x] = ca, sa
            for copy in range(x, 8, rows):
                bc[g * 8 + copy, at], bs[g * 8 + copy, at] = ca, sa
    fold = np.zeros((GROUP, LANE))
    half = LANE // 2
    fold[:, :Z] = np.tile(sine(Z), (PER, 1))
    fold[:, half : half + Z] = fold[:, :Z]
    unfold = np.zeros((2, LANE, GROUP))
    unfold[0, :Z] = fold[:, :Z].T
    unfold[1, half : half + Z] = fold[:, :Z].T
    table = sine(total)
    into = np.zeros((block * total, space * piece))
    back = np.zeros((space, 2 * piece, block * total))
    field = np.zeros((total, total))
    for x in range(total):
        if x > 0:
            field[x] += 0.5 * table[x - 1]
        if x < total - 1:
            field[x] -= 0.5 * table[x + 1]
    lam = np.ones((energy, block * total, LANE))
    for jl in range(block):
        span = slice(jl * total, (jl + 1) * total)
        for sl in range(space):
            for x in range(rows):
                into[span, sl * piece + jl * rows + x] = table[sl * rows + x]
                back[sl, jl * rows + x, span] = table[sl * rows + x]
                back[sl, piece + jl * rows + x, span] = field[sl * rows + x]
        for q in range(energy):
            lam[q, span, :Z] = 1.0 / (
                eigen(total)[:, None] + eigen(Y)[q * block + jl] + eigen(Z)[None, :]
            )
            lam[q, span, half : half + Z] = lam[q, span, :Z]
    depth = np.arange(Y * Z) % Z
    zmask = np.zeros((2, 8, Y * Z))
    zmask[0] = depth > 0
    zmask[1] = depth < Z - 1
    values = dict(
        pick=pick, pick_t=pick.T, pick_edge=pick_edge, masks=masks, mask_edge=mask_edge,
        choose=choose, dense=dense, pick_level=pick_level,
        pick_level_t=pick_level.T, fc=fc, fs=fs, bc=bc, bs=bs, cos_in=cos_in,
        sin_in=sin_in, fold=fold, unfold=unfold, into=into, back=back, lam=lam, zmask=zmask,
    )
    values = {name: np.ascontiguousarray(value, f32) for name, value in values.items()}
    return values


def dot32(a, b):
    return jnp.dot(a, b, precision=highest, preferred_element_type=jnp.float32)


def split(a):
    high = a.astype(jnp.bfloat16)
    return high, (a - high.astype(jnp.float32)).astype(jnp.bfloat16)


def dot3(a, b):
    (ah, al), (bh, bl) = split(a), split(b)
    return dot16(ah, bh) + (dot16(ah, bl) + dot16(al, bh))


def dot16(a, b):
    return jnp.dot(a, b, preferred_element_type=jnp.float32)


def kernel(names, energy, space, rows, scale, *refs):
    inputs = len(names) + 8
    held_in = refs[inputs + 2 : 2 * inputs + 2]
    c = dict(zip(names, held_in))
    (given, region, contact, doping, coupling, level_coef_t, phonon, out_rate) = held_in[
        len(names) :
    ]
    out, potential = refs[inputs : inputs + 2]
    (state, above, below, edge_out, edge_in, mix, mix_edge, total, pulls, charge, folded, modes, got1, part,
     got2, answer, got3, field, contact8, isem, ssem, rsem, esend, erecv, s1, r1, s2, r2, s3, r3) = refs[
        2 * inputs + 2 :
    ]
    padded, cells = above.shape
    edge = edge_in.shape[0] // 2
    piece = modes.shape[1]
    groups = cells // GROUP
    me = lax.axis_index("energy")
    slab = lax.axis_index("space")

    barrier = pltpu.get_barrier_semaphore()

    @pl.loop(1, energy)
    def _(o):
        pl.semaphore_signal(
            barrier, inc=1, device_id={"energy": lax.rem(me + o, energy)}, device_id_type=MESH
        )

    @pl.loop(1, space)
    def _(o):
        pl.semaphore_signal(
            barrier, inc=1, device_id={"space": lax.rem(slab + o, space)}, device_id_type=MESH
        )

    def load(i):
        return pltpu.make_async_copy(refs[i], held_in[i], isem.at[i])

    order = [len(names)] + [i for i in range(inputs) if i != len(names)]
    for i in order:
        load(i).start()

    def lanes(g):
        return pl.ds(pl.multiple_of(g * GROUP, LANE), GROUP)

    def inside(g):
        return pl.ds(pl.multiple_of(g * GROUP + LANE, LANE), GROUP)

    def level_copy(g, up):
        target = jnp.minimum(me + 1, energy - 1) if up else jnp.maximum(me - 1, 0)
        return pltpu.make_async_remote_copy(
            src_ref=state.at[:, inside(g)],
            dst_ref=(below if up else above).at[:, lanes(g)],
            send_sem=ssem.at[int(up), g],
            recv_sem=rsem.at[int(up), g],
            device_id={"energy": target},
            device_id_type=MESH,
        )

    def send_levels(first, last):
        @pl.loop(first, last)
        def _(g):
            @pl.when(me < energy - 1)
            def _():
                level_copy(g, True).start()

            @pl.when(me > 0)
            def _():
                level_copy(g, False).start()

    state[:, 0:LANE] = jnp.zeros((padded, LANE), jnp.bfloat16)
    state[:, cells + LANE :] = jnp.zeros((padded, LANE), jnp.bfloat16)
    count = given.shape[0] * rows
    load(order[0]).wait()

    @pl.loop(0, groups)
    def _(g):
        block = given[:, :, lanes(g)].astype(jnp.float32).reshape(count, GROUP)
        block = jnp.concatenate([block, jnp.zeros((padded - count, GROUP), jnp.float32)], axis=0)
        state[:, inside(g)] = block.astype(jnp.bfloat16)

    first, second, third = groups // 4, groups // 2, groups * 5 // 8
    pl.semaphore_wait(barrier, energy + space - 2)
    send_levels(0, first)
    for i in order[1:]:
        load(i).wait()

    density = dot32(level_coef_t[...], c["pick_level_t"][...])[2:3, :]
    weight = c["dense"][...] * density * scale
    high = weight.astype(jnp.bfloat16)
    rest = weight - high.astype(jnp.float32)
    middle = rest.astype(jnp.bfloat16)
    low = (rest - middle.astype(jnp.float32)).astype(jnp.bfloat16)
    weights = jnp.concatenate([high, middle, low, jnp.zeros_like(low)], axis=0)
    mine = jnp.where(me == 0, 1.0, 0.0).astype(jnp.float32)

    charge[...] = jnp.zeros_like(charge)
    for row in range(0, 8, rows):
        contact8[row : row + rows, :] = contact[...].astype(jnp.float32)
    found = jnp.zeros(region.shape, jnp.float32)
    for kind in range(doping.shape[1]):
        found = found + jnp.where(region[...] == kind, doping[0:1, kind : kind + 1], 0.0)
    charge[0:rows, :] = -found * mine
    for g in range(groups):
        span = slice(g * GROUP, (g + 1) * GROUP)
        block = state[:, g * GROUP + LANE : (g + 1) * GROUP + LANE]
        parts = dot16(weights, block)
        folded[g * 8 : (g + 1) * 8, :] = parts[0:8] + (parts[8:16] + parts[16:24]) + charge[:, span]

    def edge_copy(up):
        target = jnp.minimum(slab + 1, space - 1) if up else jnp.maximum(slab - 1, 0)
        src = pl.ds(edge, edge) if up else pl.ds(0, edge)
        dst = pl.ds(0, edge) if up else pl.ds(edge, edge)
        return pltpu.make_async_remote_copy(
            src_ref=edge_out.at[src],
            dst_ref=edge_in.at[dst],
            send_sem=esend.at[int(up)],
            recv_sem=erecv.at[int(up)],
            device_id={"space": target},
            device_id_type=MESH,
        )

    charges = folded[...]
    turned = c["sin_in"][...] * dot3(c["fc"][...], charges) + c["cos_in"][...] * dot3(
        c["fs"][...], charges
    )
    modes[...] = dot3(turned, c["fold"][...]).reshape(modes.shape)

    def spread(source, fixed, got, sends, recvs, o, sending):
        other = lax.rem(me + o, energy) if sending else lax.rem(me + energy - o, energy)
        return pltpu.make_async_remote_copy(
            src_ref=source if fixed else source.at[other],
            dst_ref=got.at[me if sending else other],
            send_sem=sends.at[o],
            recv_sem=recvs.at[me if sending else other],
            device_id={"energy": other},
            device_id_type=MESH,
        )

    @pl.loop(1, energy)
    def _(o):
        spread(modes, False, got1, s1, r1, o, True).start()

    send_levels(first, second)

    choose = c["choose"][...].astype(jnp.bfloat16)

    @pl.loop(0, groups)
    def _(g):
        edge_out[:, lanes(g)] = dot16(choose, state[:, inside(g)]).astype(jnp.bfloat16)

    pick, pick_t = c["pick"][...], c["pick_t"][...]
    slots = (0, 5, 1, 2, 3, 4)
    for d in range(6):
        wide = dot16(pick, coupling[d % 3].astype(jnp.float32)[:, d // 3, :])
        mask = c["masks"][0 if d == 0 else 1 if d < 3 else 2]
        mix[slots[d] * padded : (slots[d] + 1) * padded, :] = (dot16(wide, pick_t) * mask).astype(jnp.bfloat16)
        if d == 0:
            mix_edge[...] = (dot16(wide, c["pick_edge"][...]) * c["mask_edge"][...]).astype(
                jnp.bfloat16
            )

    def by_row(values):
        return jnp.sum(dot32(c["pick_level"][...], values) * pick, axis=1, keepdims=True)

    coef = lax.dot_general(
        c["pick_level"][...],
        level_coef_t[...],
        (((1,), (1,)), ((), ())),
        precision=highest,
        preferred_element_type=jnp.float32,
    )
    speed = step_time * coef[:, 0:1]
    pull = (step_time * 3.0) * coef[:, 1:2]
    rate_up = step_time * by_row(phonon[:, 0, :])
    rate_down = step_time * by_row(phonon[:, 1, :])
    decay = by_row(out_rate[...])
    plain = 1.0 / (1.0 + step_time * decay)
    held = 1.0 / (1.0 + step_time * (decay + contact_rate)) - plain

    def mix_group(g):
        block = state[:, inside(g)]
        size = GROUP + 2 * LANE
        around = state[:, pl.ds(pl.multiple_of(g * GROUP, LANE), size)]
        ty = dot16(mix[5 * padded :], around)
        ty = (pltpu.roll(ty, size - Z, axis=1) - pltpu.roll(ty, Z, axis=1))[:, LANE : LANE + GROUP]
        mixed = dot16(mix[0 : 5 * padded], block)
        tz = mixed[padded : 2 * padded]
        tz = pltpu.roll(tz, GROUP - 1, axis=1) * c["zmask"][1, 0:1, 0:GROUP] - pltpu.roll(
            tz, 1, axis=1
        ) * c["zmask"][0, 0:1, 0:GROUP]
        total[:, lanes(g)] = block.astype(jnp.float32) - speed * (mixed[0:padded] + ty + tz)
        for d in range(3):
            pulls[d, :, lanes(g)] = mixed[(2 + d) * padded : (3 + d) * padded]

    early = groups // 4

    @pl.loop(0, early)
    def _(g):
        mix_group(g)

    @pl.loop(1, energy)
    def _(o):
        spread(modes, False, got1, s1, r1, o, False).wait_recv()

    got1[me] = modes[me]
    summed = got1[0]
    for q in range(1, energy):
        summed = summed + got1[q]
    part[...] = summed

    def pencil(o, sending):
        other = lax.rem(slab + o, space) if sending else lax.rem(slab + space - o, space)
        return pltpu.make_async_remote_copy(
            src_ref=part,
            dst_ref=got2.at[slab if sending else other],
            send_sem=s2.at[o],
            recv_sem=r2.at[slab if sending else other],
            device_id={"space": other},
            device_id_type=MESH,
        )

    @pl.loop(1, space)
    def _(o):
        pencil(o, True).start()

    send_levels(second, third)

    @pl.when(slab < space - 1)
    def _():
        edge_copy(True).start()

    @pl.when(slab > 0)
    def _():
        edge_copy(False).start()

    got2[slab] = part[...]

    @pl.loop(1, space)
    def _(o):
        pencil(o, False).wait_recv()

    spectral = dot32(c["into"][...], got2[...].reshape(space * piece, LANE)) * c["lam"][me]
    both = dot32(c["back"][slab], spectral)
    lower = lax.broadcasted_iota(jnp.int32, (piece, LANE), 1) < LANE // 2
    answer[...] = jnp.where(lower, both[0:piece], both[piece:])

    @pl.loop(1, energy)
    def _(o):
        spread(answer, True, got3, s3, r3, o, True).start()

    send_levels(third, groups)
    got3[me] = answer[...]

    @pl.loop(early, groups)
    def _(g):
        mix_group(g)

    @pl.loop(1, energy)
    def _(o):
        spread(answer, True, got3, s3, r3, o, False).wait_recv()

    for which in range(2):
        lines = dot3(got3[...].reshape(energy * piece, LANE), c["unfold"][which])
        lines = dot3(c["bs"][...], c["cos_in"][...] * lines) + dot3(
            c["bc"][...], c["sin_in"][...] * lines
        )
        for g in range(groups):
            span = slice(g * GROUP, (g + 1) * GROUP)
            if which == 0:
                charge[:, span] = lines[g * 8 : (g + 1) * 8]
            else:
                field[0, :, span] = lines[g * 8 : (g + 1) * 8]
    level = charge[...]
    potential[...] = level[0:rows]
    column = lax.broadcasted_iota(jnp.int32, level.shape, 1)
    field[1] = 0.5 * (
        jnp.where(column >= Z, pltpu.roll(level, Z, axis=1), 0.0)
        - jnp.where(column < cells - Z, pltpu.roll(level, cells - Z, axis=1), 0.0)
    )
    field[2] = 0.5 * (
        c["zmask"][0] * pltpu.roll(level, 1, axis=1)
        - c["zmask"][1] * pltpu.roll(level, cells - 1, axis=1)
    )

    @pl.when(slab > 0)
    def _():
        edge_copy(True).wait_recv()

    @pl.when(slab == 0)
    def _():
        edge_in[0:edge, :] = jnp.zeros((edge, cells), jnp.bfloat16)

    @pl.when(slab < space - 1)
    def _():
        edge_copy(False).wait_recv()

    @pl.when(slab == space - 1)
    def _():
        edge_in[edge : 2 * edge, :] = jnp.zeros((edge, cells), jnp.bfloat16)

    @pl.when(me == 0)
    def _():
        below[...] = jnp.zeros_like(below)

    @pl.when(me == energy - 1)
    def _():
        above[...] = jnp.zeros_like(above)

    def over(values):
        return values.reshape(padded // 8, 8, GROUP)

    @pl.loop(0, groups)
    def _(g):
        pulled = over(pulls[0, :, lanes(g)]) * field[0, :, lanes(g)][None]
        pulled = pulled + over(pulls[1, :, lanes(g)]) * field[1, :, lanes(g)][None]
        pulled = pulled + over(pulls[2, :, lanes(g)]) * field[2, :, lanes(g)][None]
        total[:, lanes(g)] = (
            total[:, lanes(g)]
            + pull * pulled.reshape(padded, GROUP)
            - speed * dot16(mix_edge[...], edge_in[:, lanes(g)])
        )

    @pl.loop(0, groups)
    def _(g):
        @pl.when(me > 0)
        def _():
            level_copy(g, True).wait_recv()

        @pl.when(me < energy - 1)
        def _():
            level_copy(g, False).wait_recv()

        value = (
            total[:, lanes(g)]
            + rate_up * above[:, lanes(g)].astype(jnp.float32)
            + rate_down * below[:, lanes(g)].astype(jnp.float32)
        )
        spots = jnp.broadcast_to(
            contact8[:, lanes(g)][None], (padded // 8, 8, GROUP)
        ).reshape(padded, GROUP)
        value = (value * (plain + held * spots))[0:count]
        out[:, :, lanes(g)] = value.reshape(count // rows, rows, GROUP).astype(jnp.bfloat16)

    @pl.loop(0, groups)
    def _(g):
        @pl.when(me < energy - 1)
        def _():
            level_copy(g, True).wait_send()

        @pl.when(me > 0)
        def _():
            level_copy(g, False).wait_send()

    @pl.loop(1, energy)
    def _(o):
        spread(modes, False, got1, s1, r1, o, True).wait_send()
        spread(answer, True, got3, s3, r3, o, True).wait_send()

    @pl.loop(1, space)
    def _(o):
        pencil(o, True).wait_send()

    @pl.when(slab < space - 1)
    def _():
        edge_copy(True).wait_send()

    @pl.when(slab > 0)
    def _():
        edge_copy(False).wait_send()


def local(
    energy,
    space,
    distribution,
    region_map,
    contact_mask,
    doping_levels,
    coupling,
    level_coef,
    phonon_kernel,
    out_rate,
):
    levels, harmonics, rows, cells = distribution.shape
    count = levels * harmonics * rows
    padded = round_up(count, 16)
    edge = round_up(levels * harmonics, 16)
    constants = tables(levels, harmonics, rows, energy, space)
    names = tuple(constants)
    piece = round_up(Y // energy * rows, 8)
    groups = cells // GROUP
    vmem = pl.BlockSpec(memory_space=pltpu.VMEM)
    operands = [jnp.asarray(constants[name]) for name in names] + [
        distribution.reshape(levels * harmonics, rows, cells),
        region_map,
        contact_mask,
        doping_levels.reshape(1, -1),
        coupling.transpose(1, 2, 0, 3),
        level_coef.T,
        phonon_kernel.transpose(1, 0, 2),
        out_rate,
    ]
    bf16, f32 = jnp.bfloat16, jnp.float32
    dma = pltpu.SemaphoreType.DMA
    out, potential = pl.pallas_call(
        functools.partial(
            kernel, names, energy, space, rows, 1.0 / math.sqrt(levels * energy)
        ),
        out_shape=(
            jax.ShapeDtypeStruct((levels * harmonics, rows, cells), bf16),
            jax.ShapeDtypeStruct((rows, cells), f32),
        ),
        in_specs=[pl.BlockSpec(memory_space=pl.ANY)] * len(operands),
        out_specs=(vmem, vmem),
        scratch_shapes=[pltpu.VMEM(value.shape, value.dtype) for value in operands]
        + [
            pltpu.VMEM((padded, cells + 2 * LANE), bf16),
            pltpu.VMEM((padded, cells), bf16),
            pltpu.VMEM((padded, cells), bf16),
            pltpu.VMEM((2 * edge, cells), bf16),
            pltpu.VMEM((2 * edge, cells), bf16),
            pltpu.VMEM((6 * padded, padded), bf16),
            pltpu.VMEM((padded, 2 * edge), bf16),
            pltpu.VMEM((padded, cells), f32),
            pltpu.VMEM((3, padded, cells), f32),
            pltpu.VMEM((8, cells), f32),
            pltpu.VMEM((groups * 8, GROUP), f32),
            pltpu.VMEM((energy, piece, LANE), f32),
            pltpu.VMEM((energy, piece, LANE), f32),
            pltpu.VMEM((piece, LANE), f32),
            pltpu.VMEM((space, piece, LANE), f32),
            pltpu.VMEM((piece, LANE), f32),
            pltpu.VMEM((energy, piece, LANE), f32),
            pltpu.VMEM((3, 8, cells), f32),
            pltpu.VMEM((8, cells), f32),
            dma((len(operands),)),
            dma((2, groups)),
            dma((2, groups)),
            dma((2,)),
            dma((2,)),
            dma((energy,)),
            dma((energy,)),
            dma((space,)),
            dma((space,)),
            dma((energy,)),
            dma((energy,)),
        ],
        compiler_params=pltpu.CompilerParams(
            collective_id=0, has_side_effects=True, vmem_limit_bytes=56 * 1024 * 1024
        ),
        cost_estimate=pl.CostEstimate(
            flops=2 * 7 * padded * padded * cells,
            bytes_accessed=8 * padded * cells,
            transcendentals=0,
        ),
    )(*operands)
    return out.reshape(distribution.shape), potential


def solution(mesh):
    return jax.shard_map(
        functools.partial(local, mesh.shape["energy"], mesh.shape["space"]),
        mesh=mesh,
        in_specs=(
            P("energy", None, "space", None),
            P("space", None),
            P("space", None),
            P(),
            P(),
            P("energy", None),
            P(None, "energy", None),
            P("energy", None),
        ),
        out_specs=(P("energy", None, "space", None), P("space", None)),
        check_vma=False,
    )
```

```python
import functools
import math

import jax
import jax.numpy as jnp
import numpy as np
from jax import lax
from jax.experimental import pallas as pl
from jax.experimental.pallas import tpu as pltpu
from jax.sharding import PartitionSpec as P

Y = 64
Z = 48
step_time = 0.4
contact_rate = 2.0
highest = lax.Precision.HIGHEST
MESH = pl.DeviceIdType.MESH
LANE = 128
GROUP = math.lcm(Z, LANE)
PER = GROUP // Z


def round_up(value, unit):
    return -(-value // unit) * unit


def sine(count):
    index = np.arange(count) + 1.0
    return math.sqrt(2.0 / (count + 1)) * np.sin(math.pi * np.outer(index, index) / (count + 1))


def eigen(count):
    return 2.0 - 2.0 * np.cos(math.pi * (np.arange(count) + 1.0) / (count + 1))


def tables(levels, harmonics, rows, energy, space):
    f32 = np.float32
    count = levels * harmonics * rows
    padded = round_up(count, 16)
    edge_count = levels * harmonics
    edge = round_up(edge_count, 16)
    r = np.arange(count)
    re, rh, rx = r // (harmonics * rows), (r // rows) % harmonics, r % rows
    s = np.arange(edge_count)
    se, sh = s // harmonics, s % harmonics
    pick = np.zeros((padded, harmonics), f32)
    pick[r, rh] = 1
    pick_level = np.zeros((padded, levels), f32)
    pick_level[r, re] = 1
    pick_edge = np.zeros((harmonics, 2 * edge), f32)
    pick_edge[sh, s] = 1
    pick_edge[sh, edge + s] = 1
    same_level = re[:, None] == re[None, :]
    masks = np.zeros((3, padded, padded), f32)
    ahead = (rx[None, :] == rx[:, None] + 1) * 0.5 - (rx[None, :] == rx[:, None] - 1) * 0.5
    masks[0, :count, :count] = same_level * ahead
    masks[1, :count, :count] = same_level * (rx[:, None] == rx[None, :]) * 0.5
    masks[2, :count, :count] = same_level * (rx[:, None] == rx[None, :])
    mask_edge = np.zeros((padded, 2 * edge), f32)
    mask_edge[:count, :edge_count] = -0.5 * (re[:, None] == se) * (rx[:, None] == 0)
    mask_edge[:count, edge : edge + edge_count] = 0.5 * (re[:, None] == se) * (rx[:, None] == rows - 1)
    choose = np.zeros((2 * edge, padded), f32)
    choose[s, s * rows] = 1
    choose[edge + s, s * rows + rows - 1] = 1
    dense = np.zeros((8, padded), f32)
    for x8 in range(rows):
        dense[x8, :count] = (rh == 0) & (rx == x8)

    groups = Y // PER
    block = Y // energy
    piece = round_up(block * rows, 8)
    total = rows * space
    theta = math.pi * (np.arange(Y) + 1.0) / (Y + 1)
    norm = math.sqrt(2.0 / (Y + 1))
    fc = np.zeros((energy * piece, groups * 8))
    fs = np.zeros((energy * piece, groups * 8))
    bc = np.zeros((groups * 8, energy * piece))
    bs = np.zeros((groups * 8, energy * piece))
    cos_in = np.zeros((energy * piece, GROUP))
    sin_in = np.zeros((energy * piece, GROUP))
    inner = np.repeat(np.arange(PER) + 1.0, Z)
    g = np.arange(groups)
    for j in range(Y):
        for x in range(rows):
            at = (j // block) * piece + (j % block) * rows + x
            cos_in[at], sin_in[at] = np.cos(inner * theta[j]), np.sin(inner * theta[j])
            ca, sa = norm * np.cos(PER * g * theta[j]), norm * np.sin(PER * g * theta[j])
            fc[at, g * 8 + x], fs[at, g * 8 + x] = ca, sa
            for copy in range(x, 8, rows):
                bc[g * 8 + copy, at], bs[g * 8 + copy, at] = ca, sa
    fold = np.zeros((GROUP, LANE))
    half = LANE // 2
    fold[:, :Z] = np.tile(sine(Z), (PER, 1))
    fold[:, half : half + Z] = fold[:, :Z]
    unfold = np.zeros((2, LANE, GROUP))
    unfold[0, :Z] = fold[:, :Z].T
    unfold[1, half : half + Z] = fold[:, :Z].T
    table = sine(total)
    into = np.zeros((block * total, space * piece))
    back = np.zeros((space, 2 * piece, block * total))
    field = np.zeros((total, total))
    for x in range(total):
        if x > 0:
            field[x] += 0.5 * table[x - 1]
        if x < total - 1:
            field[x] -= 0.5 * table[x + 1]
    lam = np.ones((energy, block * total, LANE))
    for jl in range(block):
        span = slice(jl * total, (jl + 1) * total)
        for sl in range(space):
            for x in range(rows):
                into[span, sl * piece + jl * rows + x] = table[sl * rows + x]
                back[sl, jl * rows + x, span] = table[sl * rows + x]
                back[sl, piece + jl * rows + x, span] = field[sl * rows + x]
        for q in range(energy):
            lam[q, span, :Z] = 1.0 / (
                eigen(total)[:, None] + eigen(Y)[q * block + jl] + eigen(Z)[None, :]
            )
            lam[q, span, half : half + Z] = lam[q, span, :Z]
    depth = np.arange(Y * Z) % Z
    zmask = np.zeros((2, 8, Y * Z))
    zmask[0] = depth > 0
    zmask[1] = depth < Z - 1
    values = dict(
        pick=pick, pick_t=pick.T, pick_edge=pick_edge, masks=masks, mask_edge=mask_edge,
        choose=choose, dense=dense, pick_level=pick_level,
        pick_level_t=pick_level.T, fc=fc, fs=fs, bc=bc, bs=bs, cos_in=cos_in,
        sin_in=sin_in, fold=fold, unfold=unfold, into=into, back=back, lam=lam, zmask=zmask,
    )
    values = {name: np.ascontiguousarray(value, f32) for name, value in values.items()}
    return values


def dot32(a, b):
    return jnp.dot(a, b, precision=highest, preferred_element_type=jnp.float32)


def split(a):
    high = a.astype(jnp.bfloat16)
    return high, (a - high.astype(jnp.float32)).astype(jnp.bfloat16)


def dot3(a, b):
    (ah, al), (bh, bl) = split(a), split(b)
    return dot16(ah, bh) + (dot16(ah, bl) + dot16(al, bh))


def dot16(a, b):
    return jnp.dot(a, b, preferred_element_type=jnp.float32)


def kernel(names, energy, space, rows, scale, *refs):
    inputs = len(names) + 8
    held_in = refs[inputs + 2 : 2 * inputs + 2]
    c = dict(zip(names, held_in))
    (given, region, contact, doping, coupling, level_coef_t, phonon, out_rate) = held_in[
        len(names) :
    ]
    out, potential = refs[inputs : inputs + 2]
    (state, above, below, edge_out, edge_in, mix, mix_edge, total, pulls, charge, folded, modes, got1, part,
     got2, answer, got3, field, contact8, isem, ssem, rsem, esend, erecv, s1, r1, s2, r2, s3, r3) = refs[
        2 * inputs + 2 :
    ]
    padded, cells = above.shape
    edge = edge_in.shape[0] // 2
    piece = modes.shape[1]
    groups = cells // GROUP
    me = lax.axis_index("energy")
    slab = lax.axis_index("space")

    barrier = pltpu.get_barrier_semaphore()

    @pl.loop(1, energy)
    def _(o):
        pl.semaphore_signal(
            barrier, inc=1, device_id={"energy": lax.rem(me + o, energy)}, device_id_type=MESH
        )

    @pl.loop(1, space)
    def _(o):
        pl.semaphore_signal(
            barrier, inc=1, device_id={"space": lax.rem(slab + o, space)}, device_id_type=MESH
        )

    def load(i):
        return pltpu.make_async_copy(refs[i], held_in[i], isem.at[i])

    order = [len(names)] + [i for i in range(inputs) if i != len(names)]
    for i in order:
        load(i).start()

    def lanes(g):
        return pl.ds(pl.multiple_of(g * GROUP, LANE), GROUP)

    def inside(g):
        return pl.ds(pl.multiple_of(g * GROUP + LANE, LANE), GROUP)

    def level_copy(g, up):
        target = jnp.minimum(me + 1, energy - 1) if up else jnp.maximum(me - 1, 0)
        return pltpu.make_async_remote_copy(
            src_ref=state.at[:, inside(g)],
            dst_ref=(below if up else above).at[:, lanes(g)],
            send_sem=ssem.at[int(up), g],
            recv_sem=rsem.at[int(up), g],
            device_id={"energy": target},
            device_id_type=MESH,
        )

    def send_levels(first, last):
        @pl.loop(first, last)
        def _(g):
            @pl.when(me < energy - 1)
            def _():
                level_copy(g, True).start()

            @pl.when(me > 0)
            def _():
                level_copy(g, False).start()

    state[:, 0:LANE] = jnp.zeros((padded, LANE), jnp.bfloat16)
    state[:, cells + LANE :] = jnp.zeros((padded, LANE), jnp.bfloat16)
    count = given.shape[0] * rows
    load(order[0]).wait()

    def lay_out(g):
        block = given[:, :, lanes(g)].astype(jnp.float32).reshape(count, GROUP)
        block = jnp.concatenate([block, jnp.zeros((padded - count, GROUP), jnp.float32)], axis=0)
        state[:, inside(g)] = block.astype(jnp.bfloat16)

    first, second, third = groups // 4, groups * 5 // 8, groups * 3 // 4

    @pl.loop(0, first)
    def _(g):
        lay_out(g)

    pl.semaphore_wait(barrier, energy + space - 2)
    send_levels(0, first)

    @pl.loop(first, groups)
    def _(g):
        lay_out(g)

    for i in order[1:]:
        load(i).wait()

    density = dot32(level_coef_t[...], c["pick_level_t"][...])[2:3, :]
    weight = c["dense"][...] * density * scale
    high = weight.astype(jnp.bfloat16)
    rest = weight - high.astype(jnp.float32)
    middle = rest.astype(jnp.bfloat16)
    low = (rest - middle.astype(jnp.float32)).astype(jnp.bfloat16)
    weights = jnp.concatenate([high, middle, low, jnp.zeros_like(low)], axis=0)
    mine = jnp.where(me == 0, 1.0, 0.0).astype(jnp.float32)

    charge[...] = jnp.zeros_like(charge)
    for row in range(0, 8, rows):
        contact8[row : row + rows, :] = contact[...].astype(jnp.float32)
    found = jnp.zeros(region.shape, jnp.float32)
    for kind in range(doping.shape[1]):
        found = found + jnp.where(region[...] == kind, doping[0:1, kind : kind + 1], 0.0)
    charge[0:rows, :] = -found * mine
    for g in range(groups):
        span = slice(g * GROUP, (g + 1) * GROUP)
        block = state[:, g * GROUP + LANE : (g + 1) * GROUP + LANE]
        parts = dot16(weights, block)
        folded[g * 8 : (g + 1) * 8, :] = parts[0:8] + (parts[8:16] + parts[16:24]) + charge[:, span]

    def edge_copy(up):
        target = jnp.minimum(slab + 1, space - 1) if up else jnp.maximum(slab - 1, 0)
        src = pl.ds(edge, edge) if up else pl.ds(0, edge)
        dst = pl.ds(0, edge) if up else pl.ds(edge, edge)
        return pltpu.make_async_remote_copy(
            src_ref=edge_out.at[src],
            dst_ref=edge_in.at[dst],
            send_sem=esend.at[int(up)],
            recv_sem=erecv.at[int(up)],
            device_id={"space": target},
            device_id_type=MESH,
        )

    charges = folded[...]
    turned = c["sin_in"][...] * dot3(c["fc"][...], charges) + c["cos_in"][...] * dot3(
        c["fs"][...], charges
    )
    modes[...] = dot3(turned, c["fold"][...]).reshape(modes.shape)

    def spread(source, fixed, got, sends, recvs, o, sending):
        other = lax.rem(me + o, energy) if sending else lax.rem(me + energy - o, energy)
        return pltpu.make_async_remote_copy(
            src_ref=source if fixed else source.at[other],
            dst_ref=got.at[me if sending else other],
            send_sem=sends.at[o],
            recv_sem=recvs.at[me if sending else other],
            device_id={"energy": other},
            device_id_type=MESH,
        )

    @pl.loop(1, energy)
    def _(o):
        spread(modes, False, got1, s1, r1, o, True).start()

    send_levels(first, second)

    choose = c["choose"][...].astype(jnp.bfloat16)

    @pl.loop(0, groups)
    def _(g):
        edge_out[:, lanes(g)] = dot16(choose, state[:, inside(g)]).astype(jnp.bfloat16)

    pick, pick_t = c["pick"][...], c["pick_t"][...]
    slots = (0, 5, 1, 2, 3, 4)
    for d in range(6):
        wide = dot16(pick, coupling[d % 3].astype(jnp.float32)[:, d // 3, :])
        mask = c["masks"][0 if d == 0 else 1 if d < 3 else 2]
        mix[slots[d] * padded : (slots[d] + 1) * padded, :] = (dot16(wide, pick_t) * mask).astype(jnp.bfloat16)
        if d == 0:
            mix_edge[...] = (dot16(wide, c["pick_edge"][...]) * c["mask_edge"][...]).astype(
                jnp.bfloat16
            )

    def by_row(values):
        return jnp.sum(dot32(c["pick_level"][...], values) * pick, axis=1, keepdims=True)

    coef = lax.dot_general(
        c["pick_level"][...],
        level_coef_t[...],
        (((1,), (1,)), ((), ())),
        precision=highest,
        preferred_element_type=jnp.float32,
    )
    speed = step_time * coef[:, 0:1]
    pull = (step_time * 3.0) * coef[:, 1:2]
    rate_up = step_time * by_row(phonon[:, 0, :])
    rate_down = step_time * by_row(phonon[:, 1, :])
    decay = by_row(out_rate[...])
    plain = 1.0 / (1.0 + step_time * decay)
    held = 1.0 / (1.0 + step_time * (decay + contact_rate)) - plain

    def mix_group(g):
        block = state[:, inside(g)]
        size = GROUP + 2 * LANE
        around = state[:, pl.ds(pl.multiple_of(g * GROUP, LANE), size)]
        ty = dot16(mix[5 * padded :], around)
        ty = (pltpu.roll(ty, size - Z, axis=1) - pltpu.roll(ty, Z, axis=1))[:, LANE : LANE + GROUP]
        mixed = dot16(mix[0 : 5 * padded], block)
        tz = mixed[padded : 2 * padded]
        tz = pltpu.roll(tz, GROUP - 1, axis=1) * c["zmask"][1, 0:1, 0:GROUP] - pltpu.roll(
            tz, 1, axis=1
        ) * c["zmask"][0, 0:1, 0:GROUP]
        total[:, lanes(g)] = block.astype(jnp.float32) - speed * (mixed[0:padded] + ty + tz)
        for d in range(3):
            pulls[d, :, lanes(g)] = mixed[(2 + d) * padded : (3 + d) * padded]

    early = groups // 4

    @pl.loop(0, early)
    def _(g):
        mix_group(g)

    @pl.loop(1, energy)
    def _(o):
        spread(modes, False, got1, s1, r1, o, False).wait_recv()

    got1[me] = modes[me]
    summed = got1[0]
    for q in range(1, energy):
        summed = summed + got1[q]
    part[...] = summed

    def pencil(o, sending):
        other = lax.rem(slab + o, space) if sending else lax.rem(slab + space - o, space)
        return pltpu.make_async_remote_copy(
            src_ref=part,
            dst_ref=got2.at[slab if sending else other],
            send_sem=s2.at[o],
            recv_sem=r2.at[slab if sending else other],
            device_id={"space": other},
            device_id_type=MESH,
        )

    @pl.loop(1, space)
    def _(o):
        pencil(o, True).start()

    send_levels(second, third)

    @pl.when(slab < space - 1)
    def _():
        edge_copy(True).start()

    @pl.when(slab > 0)
    def _():
        edge_copy(False).start()

    got2[slab] = part[...]

    @pl.loop(1, space)
    def _(o):
        pencil(o, False).wait_recv()

    spectral = dot32(c["into"][...], got2[...].reshape(space * piece, LANE)) * c["lam"][me]
    both = dot32(c["back"][slab], spectral)
    lower = lax.broadcasted_iota(jnp.int32, (piece, LANE), 1) < LANE // 2
    answer[...] = jnp.where(lower, both[0:piece], both[piece:])

    @pl.loop(1, energy)
    def _(o):
        spread(answer, True, got3, s3, r3, o, True).start()

    send_levels(third, groups)
    got3[me] = answer[...]

    @pl.loop(early, groups)
    def _(g):
        mix_group(g)

    @pl.loop(1, energy)
    def _(o):
        spread(answer, True, got3, s3, r3, o, False).wait_recv()

    for which in range(2):
        lines = dot3(got3[...].reshape(energy * piece, LANE), c["unfold"][which])
        lines = dot3(c["bs"][...], c["cos_in"][...] * lines) + dot3(
            c["bc"][...], c["sin_in"][...] * lines
        )
        for g in range(groups):
            span = slice(g * GROUP, (g + 1) * GROUP)
            if which == 0:
                charge[:, span] = lines[g * 8 : (g + 1) * 8]
            else:
                field[0, :, span] = lines[g * 8 : (g + 1) * 8]
    level = charge[...]
    potential[...] = level[0:rows]
    column = lax.broadcasted_iota(jnp.int32, level.shape, 1)
    field[1] = 0.5 * (
        jnp.where(column >= Z, pltpu.roll(level, Z, axis=1), 0.0)
        - jnp.where(column < cells - Z, pltpu.roll(level, cells - Z, axis=1), 0.0)
    )
    field[2] = 0.5 * (
        c["zmask"][0] * pltpu.roll(level, 1, axis=1)
        - c["zmask"][1] * pltpu.roll(level, cells - 1, axis=1)
    )

    @pl.when(slab > 0)
    def _():
        edge_copy(True).wait_recv()

    @pl.when(slab == 0)
    def _():
        edge_in[0:edge, :] = jnp.zeros((edge, cells), jnp.bfloat16)

    @pl.when(slab < space - 1)
    def _():
        edge_copy(False).wait_recv()

    @pl.when(slab == space - 1)
    def _():
        edge_in[edge : 2 * edge, :] = jnp.zeros((edge, cells), jnp.bfloat16)

    @pl.when(me == 0)
    def _():
        below[...] = jnp.zeros_like(below)

    @pl.when(me == energy - 1)
    def _():
        above[...] = jnp.zeros_like(above)

    def over(values):
        return values.reshape(padded // 8, 8, GROUP)

    @pl.loop(0, groups)
    def _(g):
        pulled = over(pulls[0, :, lanes(g)]) * field[0, :, lanes(g)][None]
        pulled = pulled + over(pulls[1, :, lanes(g)]) * field[1, :, lanes(g)][None]
        pulled = pulled + over(pulls[2, :, lanes(g)]) * field[2, :, lanes(g)][None]
        total[:, lanes(g)] = (
            total[:, lanes(g)]
            + pull * pulled.reshape(padded, GROUP)
            - speed * dot16(mix_edge[...], edge_in[:, lanes(g)])
        )

    @pl.loop(0, groups)
    def _(g):
        @pl.when(me > 0)
        def _():
            level_copy(g, True).wait_recv()

        @pl.when(me < energy - 1)
        def _():
            level_copy(g, False).wait_recv()

        value = (
            total[:, lanes(g)]
            + rate_up * above[:, lanes(g)].astype(jnp.float32)
            + rate_down * below[:, lanes(g)].astype(jnp.float32)
        )
        spots = jnp.broadcast_to(
            contact8[:, lanes(g)][None], (padded // 8, 8, GROUP)
        ).reshape(padded, GROUP)
        value = (value * (plain + held * spots))[0:count]
        out[:, :, lanes(g)] = value.reshape(count // rows, rows, GROUP).astype(jnp.bfloat16)

    @pl.loop(0, groups)
    def _(g):
        @pl.when(me < energy - 1)
        def _():
            level_copy(g, True).wait_send()

        @pl.when(me > 0)
        def _():
            level_copy(g, False).wait_send()

    @pl.loop(1, energy)
    def _(o):
        spread(modes, False, got1, s1, r1, o, True).wait_send()
        spread(answer, True, got3, s3, r3, o, True).wait_send()

    @pl.loop(1, space)
    def _(o):
        pencil(o, True).wait_send()

    @pl.when(slab < space - 1)
    def _():
        edge_copy(True).wait_send()

    @pl.when(slab > 0)
    def _():
        edge_copy(False).wait_send()


def local(
    energy,
    space,
    distribution,
    region_map,
    contact_mask,
    doping_levels,
    coupling,
    level_coef,
    phonon_kernel,
    out_rate,
):
    levels, harmonics, rows, cells = distribution.shape
    count = levels * harmonics * rows
    padded = round_up(count, 16)
    edge = round_up(levels * harmonics, 16)
    constants = tables(levels, harmonics, rows, energy, space)
    names = tuple(constants)
    piece = round_up(Y // energy * rows, 8)
    groups = cells // GROUP
    vmem = pl.BlockSpec(memory_space=pltpu.VMEM)
    operands = [jnp.asarray(constants[name]) for name in names] + [
        distribution.reshape(levels * harmonics, rows, cells),
        region_map,
        contact_mask,
        doping_levels.reshape(1, -1),
        coupling.transpose(1, 2, 0, 3),
        level_coef.T,
        phonon_kernel.transpose(1, 0, 2),
        out_rate,
    ]
    bf16, f32 = jnp.bfloat16, jnp.float32
    dma = pltpu.SemaphoreType.DMA
    out, potential = pl.pallas_call(
        functools.partial(
            kernel, names, energy, space, rows, 1.0 / math.sqrt(levels * energy)
        ),
        out_shape=(
            jax.ShapeDtypeStruct((levels * harmonics, rows, cells), bf16),
            jax.ShapeDtypeStruct((rows, cells), f32),
        ),
        in_specs=[pl.BlockSpec(memory_space=pl.ANY)] * len(operands),
        out_specs=(vmem, vmem),
        scratch_shapes=[pltpu.VMEM(value.shape, value.dtype) for value in operands]
        + [
            pltpu.VMEM((padded, cells + 2 * LANE), bf16),
            pltpu.VMEM((padded, cells), bf16),
            pltpu.VMEM((padded, cells), bf16),
            pltpu.VMEM((2 * edge, cells), bf16),
            pltpu.VMEM((2 * edge, cells), bf16),
            pltpu.VMEM((6 * padded, padded), bf16),
            pltpu.VMEM((padded, 2 * edge), bf16),
            pltpu.VMEM((padded, cells), f32),
            pltpu.VMEM((3, padded, cells), f32),
            pltpu.VMEM((8, cells), f32),
            pltpu.VMEM((groups * 8, GROUP), f32),
            pltpu.VMEM((energy, piece, LANE), f32),
            pltpu.VMEM((energy, piece, LANE), f32),
            pltpu.VMEM((piece, LANE), f32),
            pltpu.VMEM((space, piece, LANE), f32),
            pltpu.VMEM((piece, LANE), f32),
            pltpu.VMEM((energy, piece, LANE), f32),
            pltpu.VMEM((3, 8, cells), f32),
            pltpu.VMEM((8, cells), f32),
            dma((len(operands),)),
            dma((2, groups)),
            dma((2, groups)),
            dma((2,)),
            dma((2,)),
            dma((energy,)),
            dma((energy,)),
            dma((space,)),
            dma((space,)),
            dma((energy,)),
            dma((energy,)),
        ],
        compiler_params=pltpu.CompilerParams(
            collective_id=0, has_side_effects=True, vmem_limit_bytes=56 * 1024 * 1024
        ),
        cost_estimate=pl.CostEstimate(
            flops=2 * 7 * padded * padded * cells,
            bytes_accessed=8 * padded * cells,
            transcendentals=0,
        ),
    )(*operands)
    return out.reshape(distribution.shape), potential


def solution(mesh):
    return jax.shard_map(
        functools.partial(local, mesh.shape["energy"], mesh.shape["space"]),
        mesh=mesh,
        in_specs=(
            P("energy", None, "space", None),
            P("space", None),
            P("space", None),
            P(),
            P(),
            P("energy", None),
            P(None, "energy", None),
            P("energy", None),
        ),
        out_specs=(P("energy", None, "space", None), P("space", None)),
        check_vma=False,
    )
```

```python
import functools
import math

import jax
import jax.numpy as jnp
import numpy as np
from jax import lax
from jax.experimental import pallas as pl
from jax.experimental.pallas import tpu as pltpu
from jax.sharding import PartitionSpec as P

Y = 64
Z = 48
step_time = 0.4
contact_rate = 2.0
highest = lax.Precision.HIGHEST
MESH = pl.DeviceIdType.MESH
LANE = 128
GROUP = math.lcm(Z, LANE)
PER = GROUP // Z


def round_up(value, unit):
    return -(-value // unit) * unit


def sine(count):
    index = np.arange(count) + 1.0
    return math.sqrt(2.0 / (count + 1)) * np.sin(math.pi * np.outer(index, index) / (count + 1))


def eigen(count):
    return 2.0 - 2.0 * np.cos(math.pi * (np.arange(count) + 1.0) / (count + 1))


def tables(levels, harmonics, rows, energy, space):
    f32 = np.float32
    count = levels * harmonics * rows
    padded = round_up(count, 16)
    edge_count = levels * harmonics
    edge = round_up(edge_count, 16)
    r = np.arange(count)
    re, rh, rx = r // (harmonics * rows), (r // rows) % harmonics, r % rows
    s = np.arange(edge_count)
    se, sh = s // harmonics, s % harmonics
    pick = np.zeros((padded, harmonics), f32)
    pick[r, rh] = 1
    pick_level = np.zeros((padded, levels), f32)
    pick_level[r, re] = 1
    pick_edge = np.zeros((harmonics, 2 * edge), f32)
    pick_edge[sh, s] = 1
    pick_edge[sh, edge + s] = 1
    same_level = re[:, None] == re[None, :]
    masks = np.zeros((3, padded, padded), f32)
    ahead = (rx[None, :] == rx[:, None] + 1) * 0.5 - (rx[None, :] == rx[:, None] - 1) * 0.5
    masks[0, :count, :count] = same_level * ahead
    masks[1, :count, :count] = same_level * (rx[:, None] == rx[None, :]) * 0.5
    masks[2, :count, :count] = same_level * (rx[:, None] == rx[None, :])
    mask_edge = np.zeros((padded, 2 * edge), f32)
    mask_edge[:count, :edge_count] = -0.5 * (re[:, None] == se) * (rx[:, None] == 0)
    mask_edge[:count, edge : edge + edge_count] = 0.5 * (re[:, None] == se) * (rx[:, None] == rows - 1)
    choose = np.zeros((2 * edge, padded), f32)
    choose[s, s * rows] = 1
    choose[edge + s, s * rows + rows - 1] = 1
    dense = np.zeros((8, padded), f32)
    for x8 in range(rows):
        dense[x8, :count] = (rh == 0) & (rx == x8)

    groups = Y // PER
    block = Y // energy
    piece = round_up(block * rows, 8)
    total = rows * space
    theta = math.pi * (np.arange(Y) + 1.0) / (Y + 1)
    norm = math.sqrt(2.0 / (Y + 1))
    fc = np.zeros((energy * piece, groups * 8))
    fs = np.zeros((energy * piece, groups * 8))
    bc = np.zeros((groups * 8, energy * piece))
    bs = np.zeros((groups * 8, energy * piece))
    cos_in = np.zeros((energy * piece, GROUP))
    sin_in = np.zeros((energy * piece, GROUP))
    inner = np.repeat(np.arange(PER) + 1.0, Z)
    g = np.arange(groups)
    for j in range(Y):
        for x in range(rows):
            at = (j // block) * piece + (j % block) * rows + x
            cos_in[at], sin_in[at] = np.cos(inner * theta[j]), np.sin(inner * theta[j])
            ca, sa = norm * np.cos(PER * g * theta[j]), norm * np.sin(PER * g * theta[j])
            fc[at, g * 8 + x], fs[at, g * 8 + x] = ca, sa
            for copy in range(x, 8, rows):
                bc[g * 8 + copy, at], bs[g * 8 + copy, at] = ca, sa
    fold = np.zeros((GROUP, LANE))
    half = LANE // 2
    fold[:, :Z] = np.tile(sine(Z), (PER, 1))
    fold[:, half : half + Z] = fold[:, :Z]
    unfold = np.zeros((2, LANE, GROUP))
    unfold[0, :Z] = fold[:, :Z].T
    unfold[1, half : half + Z] = fold[:, :Z].T
    table = sine(total)
    into = np.zeros((block * total, space * piece))
    back = np.zeros((space, 2 * piece, block * total))
    field = np.zeros((total, total))
    for x in range(total):
        if x > 0:
            field[x] += 0.5 * table[x - 1]
        if x < total - 1:
            field[x] -= 0.5 * table[x + 1]
    lam = np.ones((energy, block * total, LANE))
    for jl in range(block):
        span = slice(jl * total, (jl + 1) * total)
        for sl in range(space):
            for x in range(rows):
                into[span, sl * piece + jl * rows + x] = table[sl * rows + x]
                back[sl, jl * rows + x, span] = table[sl * rows + x]
                back[sl, piece + jl * rows + x, span] = field[sl * rows + x]
        for q in range(energy):
            lam[q, span, :Z] = 1.0 / (
                eigen(total)[:, None] + eigen(Y)[q * block + jl] + eigen(Z)[None, :]
            )
            lam[q, span, half : half + Z] = lam[q, span, :Z]
    depth = np.arange(Y * Z) % Z
    zmask = np.zeros((2, 8, Y * Z))
    zmask[0] = depth > 0
    zmask[1] = depth < Z - 1
    values = dict(
        pick=pick, pick_t=pick.T, pick_edge=pick_edge, masks=masks, mask_edge=mask_edge,
        choose=choose, dense=dense, pick_level=pick_level,
        pick_level_t=pick_level.T, fc=fc, fs=fs, bc=bc, bs=bs, cos_in=cos_in,
        sin_in=sin_in, fold=fold, unfold=unfold, into=into, back=back, lam=lam, zmask=zmask,
    )
    values = {name: np.ascontiguousarray(value, f32) for name, value in values.items()}
    return values


def dot32(a, b):
    return jnp.dot(a, b, precision=highest, preferred_element_type=jnp.float32)


def split(a):
    high = a.astype(jnp.bfloat16)
    return high, (a - high.astype(jnp.float32)).astype(jnp.bfloat16)


def dot3(a, b):
    (ah, al), (bh, bl) = split(a), split(b)
    return dot16(ah, bh) + (dot16(ah, bl) + dot16(al, bh))


def dot16(a, b):
    return jnp.dot(a, b, preferred_element_type=jnp.float32)


def kernel(names, energy, space, rows, scale, *refs):
    inputs = len(names) + 8
    held_in = refs[inputs + 2 : 2 * inputs + 2]
    c = dict(zip(names, held_in))
    (given, region, contact, doping, coupling, level_coef_t, phonon, out_rate) = held_in[
        len(names) :
    ]
    out, potential = refs[inputs : inputs + 2]
    (state, above, below, edge_out, edge_in, mix, mix_edge, total, pulls, charge, folded, modes, got1, part,
     got2, answer, got3, field, contact8, isem, ssem, rsem, esend, erecv, s1, r1, s2, r2, s3, r3) = refs[
        2 * inputs + 2 :
    ]
    padded, cells = above.shape
    edge = edge_in.shape[0] // 2
    piece = modes.shape[1]
    groups = cells // GROUP
    me = lax.axis_index("energy")
    slab = lax.axis_index("space")

    barrier = pltpu.get_barrier_semaphore()

    @pl.loop(1, energy)
    def _(o):
        pl.semaphore_signal(
            barrier, inc=1, device_id={"energy": lax.rem(me + o, energy)}, device_id_type=MESH
        )

    @pl.loop(1, space)
    def _(o):
        pl.semaphore_signal(
            barrier, inc=1, device_id={"space": lax.rem(slab + o, space)}, device_id_type=MESH
        )

    def load(i):
        return pltpu.make_async_copy(refs[i], held_in[i], isem.at[i])

    order = [len(names)] + [i for i in range(inputs) if i != len(names)]
    for i in order:
        load(i).start()

    def lanes(g):
        return pl.ds(pl.multiple_of(g * GROUP, LANE), GROUP)

    def inside(g):
        return pl.ds(pl.multiple_of(g * GROUP + LANE, LANE), GROUP)

    def level_copy(g, up):
        target = jnp.minimum(me + 1, energy - 1) if up else jnp.maximum(me - 1, 0)
        return pltpu.make_async_remote_copy(
            src_ref=state.at[:, inside(g)],
            dst_ref=(below if up else above).at[:, lanes(g)],
            send_sem=ssem.at[int(up), g],
            recv_sem=rsem.at[int(up), g],
            device_id={"energy": target},
            device_id_type=MESH,
        )

    def send_levels(first, last):
        @pl.loop(first, last)
        def _(g):
            @pl.when(me < energy - 1)
            def _():
                level_copy(g, True).start()

            @pl.when(me > 0)
            def _():
                level_copy(g, False).start()

    state[:, 0:LANE] = jnp.zeros((padded, LANE), jnp.bfloat16)
    state[:, cells + LANE :] = jnp.zeros((padded, LANE), jnp.bfloat16)
    count = given.shape[0] * rows
    load(order[0]).wait()

    def lay_out(g):
        block = given[:, :, lanes(g)].astype(jnp.float32).reshape(count, GROUP)
        block = jnp.concatenate([block, jnp.zeros((padded - count, GROUP), jnp.float32)], axis=0)
        state[:, inside(g)] = block.astype(jnp.bfloat16)

    first, second, third = groups // 4, groups * 3 // 8, groups // 2

    @pl.loop(0, first)
    def _(g):
        lay_out(g)

    pl.semaphore_wait(barrier, energy + space - 2)
    send_levels(0, first)

    @pl.loop(first, groups)
    def _(g):
        lay_out(g)

    for i in order[1:]:
        load(i).wait()

    density = dot32(level_coef_t[...], c["pick_level_t"][...])[2:3, :]
    weight = c["dense"][...] * density * scale
    high = weight.astype(jnp.bfloat16)
    rest = weight - high.astype(jnp.float32)
    middle = rest.astype(jnp.bfloat16)
    low = (rest - middle.astype(jnp.float32)).astype(jnp.bfloat16)
    weights = jnp.concatenate([high, middle, low, jnp.zeros_like(low)], axis=0)
    mine = jnp.where(me == 0, 1.0, 0.0).astype(jnp.float32)

    charge[...] = jnp.zeros_like(charge)
    for row in range(0, 8, rows):
        contact8[row : row + rows, :] = contact[...].astype(jnp.float32)
    found = jnp.zeros(region.shape, jnp.float32)
    for kind in range(doping.shape[1]):
        found = found + jnp.where(region[...] == kind, doping[0:1, kind : kind + 1], 0.0)
    charge[0:rows, :] = -found * mine
    for g in range(groups):
        span = slice(g * GROUP, (g + 1) * GROUP)
        block = state[:, g * GROUP + LANE : (g + 1) * GROUP + LANE]
        parts = dot16(weights, block)
        folded[g * 8 : (g + 1) * 8, :] = parts[0:8] + (parts[8:16] + parts[16:24]) + charge[:, span]

    def edge_copy(up):
        target = jnp.minimum(slab + 1, space - 1) if up else jnp.maximum(slab - 1, 0)
        src = pl.ds(edge, edge) if up else pl.ds(0, edge)
        dst = pl.ds(0, edge) if up else pl.ds(edge, edge)
        return pltpu.make_async_remote_copy(
            src_ref=edge_out.at[src],
            dst_ref=edge_in.at[dst],
            send_sem=esend.at[int(up)],
            recv_sem=erecv.at[int(up)],
            device_id={"space": target},
            device_id_type=MESH,
        )

    charges = folded[...]
    turned = c["sin_in"][...] * dot3(c["fc"][...], charges) + c["cos_in"][...] * dot3(
        c["fs"][...], charges
    )
    modes[...] = dot3(turned, c["fold"][...]).reshape(modes.shape)

    def spread(source, fixed, got, sends, recvs, o, sending):
        other = lax.rem(me + o, energy) if sending else lax.rem(me + energy - o, energy)
        return pltpu.make_async_remote_copy(
            src_ref=source if fixed else source.at[other],
            dst_ref=got.at[me if sending else other],
            send_sem=sends.at[o],
            recv_sem=recvs.at[me if sending else other],
            device_id={"energy": other},
            device_id_type=MESH,
        )

    @pl.loop(1, energy)
    def _(o):
        spread(modes, False, got1, s1, r1, o, True).start()

    send_levels(first, second)

    choose = c["choose"][...].astype(jnp.bfloat16)

    @pl.loop(0, groups)
    def _(g):
        edge_out[:, lanes(g)] = dot16(choose, state[:, inside(g)]).astype(jnp.bfloat16)

    pick, pick_t = c["pick"][...], c["pick_t"][...]
    slots = (0, 5, 1, 2, 3, 4)
    for d in range(6):
        wide = dot16(pick, coupling[d % 3].astype(jnp.float32)[:, d // 3, :])
        mask = c["masks"][0 if d == 0 else 1 if d < 3 else 2]
        mix[slots[d] * padded : (slots[d] + 1) * padded, :] = (dot16(wide, pick_t) * mask).astype(jnp.bfloat16)
        if d == 0:
            mix_edge[...] = (dot16(wide, c["pick_edge"][...]) * c["mask_edge"][...]).astype(
                jnp.bfloat16
            )

    def by_row(values):
        return jnp.sum(dot32(c["pick_level"][...], values) * pick, axis=1, keepdims=True)

    coef = lax.dot_general(
        c["pick_level"][...],
        level_coef_t[...],
        (((1,), (1,)), ((), ())),
        precision=highest,
        preferred_element_type=jnp.float32,
    )
    speed = step_time * coef[:, 0:1]
    pull = (step_time * 3.0) * coef[:, 1:2]
    rate_up = step_time * by_row(phonon[:, 0, :])
    rate_down = step_time * by_row(phonon[:, 1, :])
    decay = by_row(out_rate[...])
    plain = 1.0 / (1.0 + step_time * decay)
    held = 1.0 / (1.0 + step_time * (decay + contact_rate)) - plain

    def mix_group(g):
        block = state[:, inside(g)]
        size = GROUP + 2 * LANE
        around = state[:, pl.ds(pl.multiple_of(g * GROUP, LANE), size)]
        ty = dot16(mix[5 * padded :], around)
        ty = (pltpu.roll(ty, size - Z, axis=1) - pltpu.roll(ty, Z, axis=1))[:, LANE : LANE + GROUP]
        mixed = dot16(mix[0 : 5 * padded], block)
        tz = mixed[padded : 2 * padded]
        tz = pltpu.roll(tz, GROUP - 1, axis=1) * c["zmask"][1, 0:1, 0:GROUP] - pltpu.roll(
            tz, 1, axis=1
        ) * c["zmask"][0, 0:1, 0:GROUP]
        total[:, lanes(g)] = block.astype(jnp.float32) - speed * (mixed[0:padded] + ty + tz)
        for d in range(3):
            pulls[d, :, lanes(g)] = mixed[(2 + d) * padded : (3 + d) * padded]

    early = groups // 4

    @pl.loop(0, early)
    def _(g):
        mix_group(g)

    @pl.loop(1, energy)
    def _(o):
        spread(modes, False, got1, s1, r1, o, False).wait_recv()

    got1[me] = modes[me]
    summed = got1[0]
    for q in range(1, energy):
        summed = summed + got1[q]
    part[...] = summed

    def pencil(o, sending):
        other = lax.rem(slab + o, space) if sending else lax.rem(slab + space - o, space)
        return pltpu.make_async_remote_copy(
            src_ref=part,
            dst_ref=got2.at[slab if sending else other],
            send_sem=s2.at[o],
            recv_sem=r2.at[slab if sending else other],
            device_id={"space": other},
            device_id_type=MESH,
        )

    @pl.loop(1, space)
    def _(o):
        pencil(o, True).start()

    send_levels(second, third)

    @pl.when(slab < space - 1)
    def _():
        edge_copy(True).start()

    @pl.when(slab > 0)
    def _():
        edge_copy(False).start()

    got2[slab] = part[...]

    @pl.loop(1, space)
    def _(o):
        pencil(o, False).wait_recv()

    spectral = dot32(c["into"][...], got2[...].reshape(space * piece, LANE)) * c["lam"][me]
    both = dot32(c["back"][slab], spectral)
    lower = lax.broadcasted_iota(jnp.int32, (piece, LANE), 1) < LANE // 2
    answer[...] = jnp.where(lower, both[0:piece], both[piece:])

    @pl.loop(1, energy)
    def _(o):
        spread(answer, True, got3, s3, r3, o, True).start()

    send_levels(third, groups)
    got3[me] = answer[...]

    @pl.loop(early, groups)
    def _(g):
        mix_group(g)

    @pl.when(slab > 0)
    def _():
        edge_copy(True).wait_recv()

    @pl.when(slab == 0)
    def _():
        edge_in[0:edge, :] = jnp.zeros((edge, cells), jnp.bfloat16)

    @pl.when(slab < space - 1)
    def _():
        edge_copy(False).wait_recv()

    @pl.when(slab == space - 1)
    def _():
        edge_in[edge : 2 * edge, :] = jnp.zeros((edge, cells), jnp.bfloat16)

    @pl.when(me == 0)
    def _():
        below[...] = jnp.zeros_like(below)

    @pl.when(me == energy - 1)
    def _():
        above[...] = jnp.zeros_like(above)

    @pl.loop(0, groups)
    def _(g):
        total[:, lanes(g)] -= speed * dot16(mix_edge[...], edge_in[:, lanes(g)])

    @pl.loop(1, energy)
    def _(o):
        spread(answer, True, got3, s3, r3, o, False).wait_recv()

    for which in range(2):
        lines = dot3(got3[...].reshape(energy * piece, LANE), c["unfold"][which])
        lines = dot3(c["bs"][...], c["cos_in"][...] * lines) + dot3(
            c["bc"][...], c["sin_in"][...] * lines
        )
        for g in range(groups):
            span = slice(g * GROUP, (g + 1) * GROUP)
            if which == 0:
                charge[:, span] = lines[g * 8 : (g + 1) * 8]
            else:
                field[0, :, span] = lines[g * 8 : (g + 1) * 8]
    level = charge[...]
    potential[...] = level[0:rows]
    column = lax.broadcasted_iota(jnp.int32, level.shape, 1)
    field[1] = 0.5 * (
        jnp.where(column >= Z, pltpu.roll(level, Z, axis=1), 0.0)
        - jnp.where(column < cells - Z, pltpu.roll(level, cells - Z, axis=1), 0.0)
    )
    field[2] = 0.5 * (
        c["zmask"][0] * pltpu.roll(level, 1, axis=1)
        - c["zmask"][1] * pltpu.roll(level, cells - 1, axis=1)
    )

    def over(values):
        return values.reshape(padded // 8, 8, GROUP)

    @pl.loop(0, groups)
    def _(g):
        pulled = over(pulls[0, :, lanes(g)]) * field[0, :, lanes(g)][None]
        pulled = pulled + over(pulls[1, :, lanes(g)]) * field[1, :, lanes(g)][None]
        pulled = pulled + over(pulls[2, :, lanes(g)]) * field[2, :, lanes(g)][None]

        @pl.when(me > 0)
        def _():
            level_copy(g, True).wait_recv()

        @pl.when(me < energy - 1)
        def _():
            level_copy(g, False).wait_recv()

        value = (
            total[:, lanes(g)]
            + pull * pulled.reshape(padded, GROUP)
            + rate_up * above[:, lanes(g)].astype(jnp.float32)
            + rate_down * below[:, lanes(g)].astype(jnp.float32)
        )
        spots = jnp.broadcast_to(
            contact8[:, lanes(g)][None], (padded // 8, 8, GROUP)
        ).reshape(padded, GROUP)
        value = (value * (plain + held * spots))[0:count]
        out[:, :, lanes(g)] = value.reshape(count // rows, rows, GROUP).astype(jnp.bfloat16)

    @pl.loop(0, groups)
    def _(g):
        @pl.when(me < energy - 1)
        def _():
            level_copy(g, True).wait_send()

        @pl.when(me > 0)
        def _():
            level_copy(g, False).wait_send()

    @pl.loop(1, energy)
    def _(o):
        spread(modes, False, got1, s1, r1, o, True).wait_send()
        spread(answer, True, got3, s3, r3, o, True).wait_send()

    @pl.loop(1, space)
    def _(o):
        pencil(o, True).wait_send()

    @pl.when(slab < space - 1)
    def _():
        edge_copy(True).wait_send()

    @pl.when(slab > 0)
    def _():
        edge_copy(False).wait_send()


def local(
    energy,
    space,
    distribution,
    region_map,
    contact_mask,
    doping_levels,
    coupling,
    level_coef,
    phonon_kernel,
    out_rate,
):
    levels, harmonics, rows, cells = distribution.shape
    count = levels * harmonics * rows
    padded = round_up(count, 16)
    edge = round_up(levels * harmonics, 16)
    constants = tables(levels, harmonics, rows, energy, space)
    names = tuple(constants)
    piece = round_up(Y // energy * rows, 8)
    groups = cells // GROUP
    vmem = pl.BlockSpec(memory_space=pltpu.VMEM)
    operands = [jnp.asarray(constants[name]) for name in names] + [
        distribution.reshape(levels * harmonics, rows, cells),
        region_map,
        contact_mask,
        doping_levels.reshape(1, -1),
        coupling.transpose(1, 2, 0, 3),
        level_coef.T,
        phonon_kernel.transpose(1, 0, 2),
        out_rate,
    ]
    bf16, f32 = jnp.bfloat16, jnp.float32
    dma = pltpu.SemaphoreType.DMA
    out, potential = pl.pallas_call(
        functools.partial(
            kernel, names, energy, space, rows, 1.0 / math.sqrt(levels * energy)
        ),
        out_shape=(
            jax.ShapeDtypeStruct((levels * harmonics, rows, cells), bf16),
            jax.ShapeDtypeStruct((rows, cells), f32),
        ),
        in_specs=[pl.BlockSpec(memory_space=pl.ANY)] * len(operands),
        out_specs=(vmem, vmem),
        scratch_shapes=[pltpu.VMEM(value.shape, value.dtype) for value in operands]
        + [
            pltpu.VMEM((padded, cells + 2 * LANE), bf16),
            pltpu.VMEM((padded, cells), bf16),
            pltpu.VMEM((padded, cells), bf16),
            pltpu.VMEM((2 * edge, cells), bf16),
            pltpu.VMEM((2 * edge, cells), bf16),
            pltpu.VMEM((6 * padded, padded), bf16),
            pltpu.VMEM((padded, 2 * edge), bf16),
            pltpu.VMEM((padded, cells), f32),
            pltpu.VMEM((3, padded, cells), f32),
            pltpu.VMEM((8, cells), f32),
            pltpu.VMEM((groups * 8, GROUP), f32),
            pltpu.VMEM((energy, piece, LANE), f32),
            pltpu.VMEM((energy, piece, LANE), f32),
            pltpu.VMEM((piece, LANE), f32),
            pltpu.VMEM((space, piece, LANE), f32),
            pltpu.VMEM((piece, LANE), f32),
            pltpu.VMEM((energy, piece, LANE), f32),
            pltpu.VMEM((3, 8, cells), f32),
            pltpu.VMEM((8, cells), f32),
            dma((len(operands),)),
            dma((2, groups)),
            dma((2, groups)),
            dma((2,)),
            dma((2,)),
            dma((energy,)),
            dma((energy,)),
            dma((space,)),
            dma((space,)),
            dma((energy,)),
            dma((energy,)),
        ],
        compiler_params=pltpu.CompilerParams(
            collective_id=0, has_side_effects=True, vmem_limit_bytes=56 * 1024 * 1024
        ),
        cost_estimate=pl.CostEstimate(
            flops=2 * 7 * padded * padded * cells,
            bytes_accessed=8 * padded * cells,
            transcendentals=0,
        ),
    )(*operands)
    return out.reshape(distribution.shape), potential


def solution(mesh):
    return jax.shard_map(
        functools.partial(local, mesh.shape["energy"], mesh.shape["space"]),
        mesh=mesh,
        in_specs=(
            P("energy", None, "space", None),
            P("space", None),
            P("space", None),
            P(),
            P(),
            P("energy", None),
            P(None, "energy", None),
            P("energy", None),
        ),
        out_specs=(P("energy", None, "space", None), P("space", None)),
        check_vma=False,
    )
```

```python
import functools
import math

import jax
import jax.numpy as jnp
import numpy as np
from jax import lax
from jax.experimental import pallas as pl
from jax.experimental.pallas import tpu as pltpu
from jax.sharding import PartitionSpec as P

Y = 64
Z = 48
step_time = 0.4
contact_rate = 2.0
highest = lax.Precision.HIGHEST
MESH = pl.DeviceIdType.MESH
LANE = 128
GROUP = math.lcm(Z, LANE)
PER = GROUP // Z


def round_up(value, unit):
    return -(-value // unit) * unit


def sine(count):
    index = np.arange(count) + 1.0
    return math.sqrt(2.0 / (count + 1)) * np.sin(math.pi * np.outer(index, index) / (count + 1))


def eigen(count):
    return 2.0 - 2.0 * np.cos(math.pi * (np.arange(count) + 1.0) / (count + 1))


def tables(levels, harmonics, rows, energy, space):
    f32 = np.float32
    count = levels * harmonics * rows
    padded = round_up(count, 16)
    edge_count = levels * harmonics
    edge = round_up(edge_count, 16)
    r = np.arange(count)
    re, rh, rx = r // (harmonics * rows), (r // rows) % harmonics, r % rows
    s = np.arange(edge_count)
    se, sh = s // harmonics, s % harmonics
    pick = np.zeros((padded, harmonics), f32)
    pick[r, rh] = 1
    pick_level = np.zeros((padded, levels), f32)
    pick_level[r, re] = 1
    pick_edge = np.zeros((harmonics, 2 * edge), f32)
    pick_edge[sh, s] = 1
    pick_edge[sh, edge + s] = 1
    same_level = re[:, None] == re[None, :]
    masks = np.zeros((3, padded, padded), f32)
    ahead = (rx[None, :] == rx[:, None] + 1) * 0.5 - (rx[None, :] == rx[:, None] - 1) * 0.5
    masks[0, :count, :count] = same_level * ahead
    masks[1, :count, :count] = same_level * (rx[:, None] == rx[None, :]) * 0.5
    masks[2, :count, :count] = same_level * (rx[:, None] == rx[None, :])
    mask_edge = np.zeros((padded, 2 * edge), f32)
    mask_edge[:count, :edge_count] = -0.5 * (re[:, None] == se) * (rx[:, None] == 0)
    mask_edge[:count, edge : edge + edge_count] = 0.5 * (re[:, None] == se) * (rx[:, None] == rows - 1)
    choose = np.zeros((2 * edge, padded), f32)
    choose[s, s * rows] = 1
    choose[edge + s, s * rows + rows - 1] = 1
    dense = np.zeros((8, padded), f32)
    for x8 in range(rows):
        dense[x8, :count] = (rh == 0) & (rx == x8)

    groups = Y // PER
    block = Y // energy
    piece = round_up(block * rows, 8)
    total = rows * space
    theta = math.pi * (np.arange(Y) + 1.0) / (Y + 1)
    norm = math.sqrt(2.0 / (Y + 1))
    fc = np.zeros((energy * piece, groups * 8))
    fs = np.zeros((energy * piece, groups * 8))
    bc = np.zeros((groups * 8, energy * piece))
    bs = np.zeros((groups * 8, energy * piece))
    cos_in = np.zeros((energy * piece, GROUP))
    sin_in = np.zeros((energy * piece, GROUP))
    inner = np.repeat(np.arange(PER) + 1.0, Z)
    g = np.arange(groups)
    for j in range(Y):
        for x in range(rows):
            at = (j // block) * piece + (j % block) * rows + x
            cos_in[at], sin_in[at] = np.cos(inner * theta[j]), np.sin(inner * theta[j])
            ca, sa = norm * np.cos(PER * g * theta[j]), norm * np.sin(PER * g * theta[j])
            fc[at, g * 8 + x], fs[at, g * 8 + x] = ca, sa
            for copy in range(x, 8, rows):
                bc[g * 8 + copy, at], bs[g * 8 + copy, at] = ca, sa
    fold = np.zeros((GROUP, LANE))
    half = LANE // 2
    fold[:, :Z] = np.tile(sine(Z), (PER, 1))
    fold[:, half : half + Z] = fold[:, :Z]
    unfold = np.zeros((2, LANE, GROUP))
    unfold[0, :Z] = fold[:, :Z].T
    unfold[1, half : half + Z] = fold[:, :Z].T
    table = sine(total)
    into = np.zeros((block * total, space * piece))
    back = np.zeros((space, 2 * piece, block * total))
    field = np.zeros((total, total))
    for x in range(total):
        if x > 0:
            field[x] += 0.5 * table[x - 1]
        if x < total - 1:
            field[x] -= 0.5 * table[x + 1]
    lam = np.ones((energy, block * total, LANE))
    for jl in range(block):
        span = slice(jl * total, (jl + 1) * total)
        for sl in range(space):
            for x in range(rows):
                into[span, sl * piece + jl * rows + x] = table[sl * rows + x]
                back[sl, jl * rows + x, span] = table[sl * rows + x]
                back[sl, piece + jl * rows + x, span] = field[sl * rows + x]
        for q in range(energy):
            lam[q, span, :Z] = 1.0 / (
                eigen(total)[:, None] + eigen(Y)[q * block + jl] + eigen(Z)[None, :]
            )
            lam[q, span, half : half + Z] = lam[q, span, :Z]
    depth = np.arange(Y * Z) % Z
    zmask = np.zeros((2, 8, Y * Z))
    zmask[0] = depth > 0
    zmask[1] = depth < Z - 1
    values = dict(
        pick=pick, pick_t=pick.T, pick_edge=pick_edge, masks=masks, mask_edge=mask_edge,
        choose=choose, dense=dense, pick_level=pick_level,
        pick_level_t=pick_level.T, fc=fc, fs=fs, bc=bc, bs=bs, cos_in=cos_in,
        sin_in=sin_in, fold=fold, unfold=unfold, into=into, back=back, lam=lam, zmask=zmask,
    )
    values = {name: np.ascontiguousarray(value, f32) for name, value in values.items()}
    return values


def dot32(a, b):
    return jnp.dot(a, b, precision=highest, preferred_element_type=jnp.float32)


def split(a):
    high = a.astype(jnp.bfloat16)
    return high, (a - high.astype(jnp.float32)).astype(jnp.bfloat16)


def dot3(a, b):
    (ah, al), (bh, bl) = split(a), split(b)
    return dot16(ah, bh) + (dot16(ah, bl) + dot16(al, bh))


def dot16(a, b):
    return jnp.dot(a, b, preferred_element_type=jnp.float32)


def kernel(names, energy, space, rows, scale, *refs):
    inputs = len(names) + 8
    held_in = refs[inputs + 2 : 2 * inputs + 2]
    c = dict(zip(names, held_in))
    (given, region, contact, doping, coupling, level_coef_t, phonon, out_rate) = held_in[
        len(names) :
    ]
    out, potential = refs[inputs : inputs + 2]
    (state, above, below, edge_out, edge_in, mix, mix_edge, total, pulls, charge, folded, modes, got1, part,
     got2, answer, got3, field, contact8, isem, ssem, rsem, esend, erecv, s1, r1, s2, r2, s3, r3) = refs[
        2 * inputs + 2 :
    ]
    padded, cells = above.shape
    edge = edge_in.shape[0] // 2
    piece = modes.shape[1]
    groups = cells // GROUP
    me = lax.axis_index("energy")
    slab = lax.axis_index("space")

    barrier = pltpu.get_barrier_semaphore()

    @pl.loop(1, energy)
    def _(o):
        pl.semaphore_signal(
            barrier, inc=1, device_id={"energy": lax.rem(me + o, energy)}, device_id_type=MESH
        )

    @pl.loop(1, space)
    def _(o):
        pl.semaphore_signal(
            barrier, inc=1, device_id={"space": lax.rem(slab + o, space)}, device_id_type=MESH
        )

    def load(i):
        return pltpu.make_async_copy(refs[i], held_in[i], isem.at[i])

    order = [len(names)] + [i for i in range(inputs) if i != len(names)]
    for i in order:
        load(i).start()

    def lanes(g):
        return pl.ds(pl.multiple_of(g * GROUP, LANE), GROUP)

    def inside(g):
        return pl.ds(pl.multiple_of(g * GROUP + LANE, LANE), GROUP)

    def level_copy(g, up):
        target = jnp.minimum(me + 1, energy - 1) if up else jnp.maximum(me - 1, 0)
        return pltpu.make_async_remote_copy(
            src_ref=state.at[:, inside(g)],
            dst_ref=(below if up else above).at[:, lanes(g)],
            send_sem=ssem.at[int(up), g],
            recv_sem=rsem.at[int(up), g],
            device_id={"energy": target},
            device_id_type=MESH,
        )

    odd = lax.rem(me, 2)

    def send_levels(first, last, outward=True):
        @pl.loop(first, last)
        def _(g):
            @pl.when((me < energy - 1) & (odd == (1 if outward else 0)))
            def _():
                level_copy(g, True).start()

            @pl.when((me > 0) & (odd == (0 if outward else 1)))
            def _():
                level_copy(g, False).start()

    state[:, 0:LANE] = jnp.zeros((padded, LANE), jnp.bfloat16)
    state[:, cells + LANE :] = jnp.zeros((padded, LANE), jnp.bfloat16)
    count = given.shape[0] * rows
    load(order[0]).wait()

    def lay_out(g):
        block = given[:, :, lanes(g)].astype(jnp.float32).reshape(count, GROUP)
        block = jnp.concatenate([block, jnp.zeros((padded - count, GROUP), jnp.float32)], axis=0)
        state[:, inside(g)] = block.astype(jnp.bfloat16)

    first, second, third = groups // 4, groups // 2, groups * 5 // 8

    @pl.loop(0, first)
    def _(g):
        lay_out(g)

    pl.semaphore_wait(barrier, energy + space - 2)
    send_levels(0, first)

    @pl.loop(first, groups)
    def _(g):
        lay_out(g)

    for i in order[1:]:
        load(i).wait()

    density = dot32(level_coef_t[...], c["pick_level_t"][...])[2:3, :]
    weight = c["dense"][...] * density * scale
    high = weight.astype(jnp.bfloat16)
    rest = weight - high.astype(jnp.float32)
    middle = rest.astype(jnp.bfloat16)
    low = (rest - middle.astype(jnp.float32)).astype(jnp.bfloat16)
    weights = jnp.concatenate([high, middle, low, jnp.zeros_like(low)], axis=0)
    mine = jnp.where(me == 0, 1.0, 0.0).astype(jnp.float32)

    charge[...] = jnp.zeros_like(charge)
    for row in range(0, 8, rows):
        contact8[row : row + rows, :] = contact[...].astype(jnp.float32)
    found = jnp.zeros(region.shape, jnp.float32)
    for kind in range(doping.shape[1]):
        found = found + jnp.where(region[...] == kind, doping[0:1, kind : kind + 1], 0.0)
    charge[0:rows, :] = -found * mine
    for g in range(groups):
        span = slice(g * GROUP, (g + 1) * GROUP)
        block = state[:, g * GROUP + LANE : (g + 1) * GROUP + LANE]
        parts = dot16(weights, block)
        folded[g * 8 : (g + 1) * 8, :] = parts[0:8] + (parts[8:16] + parts[16:24]) + charge[:, span]

    def edge_copy(up):
        target = jnp.minimum(slab + 1, space - 1) if up else jnp.maximum(slab - 1, 0)
        src = pl.ds(edge, edge) if up else pl.ds(0, edge)
        dst = pl.ds(0, edge) if up else pl.ds(edge, edge)
        return pltpu.make_async_remote_copy(
            src_ref=edge_out.at[src],
            dst_ref=edge_in.at[dst],
            send_sem=esend.at[int(up)],
            recv_sem=erecv.at[int(up)],
            device_id={"space": target},
            device_id_type=MESH,
        )

    charges = folded[...]
    turned = c["sin_in"][...] * dot3(c["fc"][...], charges) + c["cos_in"][...] * dot3(
        c["fs"][...], charges
    )
    modes[...] = dot3(turned, c["fold"][...]).reshape(modes.shape)

    def spread(source, fixed, got, sends, recvs, o, sending):
        other = lax.rem(me + o, energy) if sending else lax.rem(me + energy - o, energy)
        return pltpu.make_async_remote_copy(
            src_ref=source if fixed else source.at[other],
            dst_ref=got.at[me if sending else other],
            send_sem=sends.at[o],
            recv_sem=recvs.at[me if sending else other],
            device_id={"energy": other},
            device_id_type=MESH,
        )

    @pl.loop(1, energy)
    def _(o):
        spread(modes, False, got1, s1, r1, o, True).start()

    send_levels(first, second)

    choose = c["choose"][...].astype(jnp.bfloat16)

    @pl.loop(0, groups)
    def _(g):
        edge_out[:, lanes(g)] = dot16(choose, state[:, inside(g)]).astype(jnp.bfloat16)

    pick, pick_t = c["pick"][...], c["pick_t"][...]
    slots = (0, 5, 1, 2, 3, 4)
    for d in range(6):
        wide = dot16(pick, coupling[d % 3].astype(jnp.float32)[:, d // 3, :])
        mask = c["masks"][0 if d == 0 else 1 if d < 3 else 2]
        mix[slots[d] * padded : (slots[d] + 1) * padded, :] = (dot16(wide, pick_t) * mask).astype(jnp.bfloat16)
        if d == 0:
            mix_edge[...] = (dot16(wide, c["pick_edge"][...]) * c["mask_edge"][...]).astype(
                jnp.bfloat16
            )

    def by_row(values):
        return jnp.sum(dot32(c["pick_level"][...], values) * pick, axis=1, keepdims=True)

    coef = lax.dot_general(
        c["pick_level"][...],
        level_coef_t[...],
        (((1,), (1,)), ((), ())),
        precision=highest,
        preferred_element_type=jnp.float32,
    )
    speed = step_time * coef[:, 0:1]
    pull = (step_time * 3.0) * coef[:, 1:2]
    rate_up = step_time * by_row(phonon[:, 0, :])
    rate_down = step_time * by_row(phonon[:, 1, :])
    decay = by_row(out_rate[...])
    plain = 1.0 / (1.0 + step_time * decay)
    held = 1.0 / (1.0 + step_time * (decay + contact_rate)) - plain

    def mix_group(g):
        block = state[:, inside(g)]
        size = GROUP + 2 * LANE
        around = state[:, pl.ds(pl.multiple_of(g * GROUP, LANE), size)]
        ty = dot16(mix[5 * padded :], around)
        ty = (pltpu.roll(ty, size - Z, axis=1) - pltpu.roll(ty, Z, axis=1))[:, LANE : LANE + GROUP]
        mixed = dot16(mix[0 : 5 * padded], block)
        tz = mixed[padded : 2 * padded]
        tz = pltpu.roll(tz, GROUP - 1, axis=1) * c["zmask"][1, 0:1, 0:GROUP] - pltpu.roll(
            tz, 1, axis=1
        ) * c["zmask"][0, 0:1, 0:GROUP]
        total[:, lanes(g)] = block.astype(jnp.float32) - speed * (mixed[0:padded] + ty + tz)
        for d in range(3):
            pulls[d, :, lanes(g)] = mixed[(2 + d) * padded : (3 + d) * padded]

    early = groups // 4

    @pl.loop(0, early)
    def _(g):
        mix_group(g)

    @pl.loop(1, energy)
    def _(o):
        spread(modes, False, got1, s1, r1, o, False).wait_recv()

    got1[me] = modes[me]
    summed = got1[0]
    for q in range(1, energy):
        summed = summed + got1[q]
    part[...] = summed

    def pencil(o, sending):
        other = lax.rem(slab + o, space) if sending else lax.rem(slab + space - o, space)
        return pltpu.make_async_remote_copy(
            src_ref=part,
            dst_ref=got2.at[slab if sending else other],
            send_sem=s2.at[o],
            recv_sem=r2.at[slab if sending else other],
            device_id={"space": other},
            device_id_type=MESH,
        )

    @pl.loop(1, space)
    def _(o):
        pencil(o, True).start()

    send_levels(second, third)

    @pl.when(slab < space - 1)
    def _():
        edge_copy(True).start()

    @pl.when(slab > 0)
    def _():
        edge_copy(False).start()

    got2[slab] = part[...]

    @pl.loop(1, space)
    def _(o):
        pencil(o, False).wait_recv()

    spectral = dot32(c["into"][...], got2[...].reshape(space * piece, LANE)) * c["lam"][me]
    both = dot32(c["back"][slab], spectral)
    lower = lax.broadcasted_iota(jnp.int32, (piece, LANE), 1) < LANE // 2
    answer[...] = jnp.where(lower, both[0:piece], both[piece:])

    @pl.loop(1, energy)
    def _(o):
        spread(answer, True, got3, s3, r3, o, True).start()

    send_levels(third, groups)
    send_levels(0, groups, False)
    got3[me] = answer[...]

    @pl.loop(early, groups)
    def _(g):
        mix_group(g)

    @pl.when(slab > 0)
    def _():
        edge_copy(True).wait_recv()

    @pl.when(slab == 0)
    def _():
        edge_in[0:edge, :] = jnp.zeros((edge, cells), jnp.bfloat16)

    @pl.when(slab < space - 1)
    def _():
        edge_copy(False).wait_recv()

    @pl.when(slab == space - 1)
    def _():
        edge_in[edge : 2 * edge, :] = jnp.zeros((edge, cells), jnp.bfloat16)

    @pl.when(me == 0)
    def _():
        below[...] = jnp.zeros_like(below)

    @pl.when(me == energy - 1)
    def _():
        above[...] = jnp.zeros_like(above)

    @pl.loop(0, groups)
    def _(g):
        total[:, lanes(g)] -= speed * dot16(mix_edge[...], edge_in[:, lanes(g)])

    @pl.loop(1, energy)
    def _(o):
        spread(answer, True, got3, s3, r3, o, False).wait_recv()

    for which in range(2):
        lines = dot3(got3[...].reshape(energy * piece, LANE), c["unfold"][which])
        lines = dot3(c["bs"][...], c["cos_in"][...] * lines) + dot3(
            c["bc"][...], c["sin_in"][...] * lines
        )
        for g in range(groups):
            span = slice(g * GROUP, (g + 1) * GROUP)
            if which == 0:
                charge[:, span] = lines[g * 8 : (g + 1) * 8]
            else:
                field[0, :, span] = lines[g * 8 : (g + 1) * 8]
    level = charge[...]
    potential[...] = level[0:rows]
    column = lax.broadcasted_iota(jnp.int32, level.shape, 1)
    field[1] = 0.5 * (
        jnp.where(column >= Z, pltpu.roll(level, Z, axis=1), 0.0)
        - jnp.where(column < cells - Z, pltpu.roll(level, cells - Z, axis=1), 0.0)
    )
    field[2] = 0.5 * (
        c["zmask"][0] * pltpu.roll(level, 1, axis=1)
        - c["zmask"][1] * pltpu.roll(level, cells - 1, axis=1)
    )

    def over(values):
        return values.reshape(padded // 8, 8, GROUP)

    @pl.loop(0, groups)
    def _(g):
        pulled = over(pulls[0, :, lanes(g)]) * field[0, :, lanes(g)][None]
        pulled = pulled + over(pulls[1, :, lanes(g)]) * field[1, :, lanes(g)][None]
        pulled = pulled + over(pulls[2, :, lanes(g)]) * field[2, :, lanes(g)][None]

        @pl.when(me > 0)
        def _():
            level_copy(g, True).wait_recv()

        @pl.when(me < energy - 1)
        def _():
            level_copy(g, False).wait_recv()

        value = (
            total[:, lanes(g)]
            + pull * pulled.reshape(padded, GROUP)
            + rate_up * above[:, lanes(g)].astype(jnp.float32)
            + rate_down * below[:, lanes(g)].astype(jnp.float32)
        )
        spots = jnp.broadcast_to(
            contact8[:, lanes(g)][None], (padded // 8, 8, GROUP)
        ).reshape(padded, GROUP)
        value = (value * (plain + held * spots))[0:count]
        out[:, :, lanes(g)] = value.reshape(count // rows, rows, GROUP).astype(jnp.bfloat16)

    @pl.loop(0, groups)
    def _(g):
        @pl.when(me < energy - 1)
        def _():
            level_copy(g, True).wait_send()

        @pl.when(me > 0)
        def _():
            level_copy(g, False).wait_send()

    @pl.loop(1, energy)
    def _(o):
        spread(modes, False, got1, s1, r1, o, True).wait_send()
        spread(answer, True, got3, s3, r3, o, True).wait_send()

    @pl.loop(1, space)
    def _(o):
        pencil(o, True).wait_send()

    @pl.when(slab < space - 1)
    def _():
        edge_copy(True).wait_send()

    @pl.when(slab > 0)
    def _():
        edge_copy(False).wait_send()


def local(
    energy,
    space,
    distribution,
    region_map,
    contact_mask,
    doping_levels,
    coupling,
    level_coef,
    phonon_kernel,
    out_rate,
):
    levels, harmonics, rows, cells = distribution.shape
    count = levels * harmonics * rows
    padded = round_up(count, 16)
    edge = round_up(levels * harmonics, 16)
    constants = tables(levels, harmonics, rows, energy, space)
    names = tuple(constants)
    piece = round_up(Y // energy * rows, 8)
    groups = cells // GROUP
    vmem = pl.BlockSpec(memory_space=pltpu.VMEM)
    operands = [jnp.asarray(constants[name]) for name in names] + [
        distribution.reshape(levels * harmonics, rows, cells),
        region_map,
        contact_mask,
        doping_levels.reshape(1, -1),
        coupling.transpose(1, 2, 0, 3),
        level_coef.T,
        phonon_kernel.transpose(1, 0, 2),
        out_rate,
    ]
    bf16, f32 = jnp.bfloat16, jnp.float32
    dma = pltpu.SemaphoreType.DMA
    out, potential = pl.pallas_call(
        functools.partial(
            kernel, names, energy, space, rows, 1.0 / math.sqrt(levels * energy)
        ),
        out_shape=(
            jax.ShapeDtypeStruct((levels * harmonics, rows, cells), bf16),
            jax.ShapeDtypeStruct((rows, cells), f32),
        ),
        in_specs=[pl.BlockSpec(memory_space=pl.ANY)] * len(operands),
        out_specs=(vmem, vmem),
        scratch_shapes=[pltpu.VMEM(value.shape, value.dtype) for value in operands]
        + [
            pltpu.VMEM((padded, cells + 2 * LANE), bf16),
            pltpu.VMEM((padded, cells), bf16),
            pltpu.VMEM((padded, cells), bf16),
            pltpu.VMEM((2 * edge, cells), bf16),
            pltpu.VMEM((2 * edge, cells), bf16),
            pltpu.VMEM((6 * padded, padded), bf16),
            pltpu.VMEM((padded, 2 * edge), bf16),
            pltpu.VMEM((padded, cells), f32),
            pltpu.VMEM((3, padded, cells), f32),
            pltpu.VMEM((8, cells), f32),
            pltpu.VMEM((groups * 8, GROUP), f32),
            pltpu.VMEM((energy, piece, LANE), f32),
            pltpu.VMEM((energy, piece, LANE), f32),
            pltpu.VMEM((piece, LANE), f32),
            pltpu.VMEM((space, piece, LANE), f32),
            pltpu.VMEM((piece, LANE), f32),
            pltpu.VMEM((energy, piece, LANE), f32),
            pltpu.VMEM((3, 8, cells), f32),
            pltpu.VMEM((8, cells), f32),
            dma((len(operands),)),
            dma((2, groups)),
            dma((2, groups)),
            dma((2,)),
            dma((2,)),
            dma((energy,)),
            dma((energy,)),
            dma((space,)),
            dma((space,)),
            dma((energy,)),
            dma((energy,)),
        ],
        compiler_params=pltpu.CompilerParams(
            collective_id=0, has_side_effects=True, vmem_limit_bytes=56 * 1024 * 1024
        ),
        cost_estimate=pl.CostEstimate(
            flops=2 * 7 * padded * padded * cells,
            bytes_accessed=8 * padded * cells,
            transcendentals=0,
        ),
    )(*operands)
    return out.reshape(distribution.shape), potential


def solution(mesh):
    return jax.shard_map(
        functools.partial(local, mesh.shape["energy"], mesh.shape["space"]),
        mesh=mesh,
        in_specs=(
            P("energy", None, "space", None),
            P("space", None),
            P("space", None),
            P(),
            P(),
            P("energy", None),
            P(None, "energy", None),
            P("energy", None),
        ),
        out_specs=(P("energy", None, "space", None), P("space", None)),
        check_vma=False,
    )
```
